32 devices in a mesh: dp: 8 (over z, x), seq: 4 (over y, core).
Axes of the slice: x: 2, y: 2, z: 4, core: 2. Of those that a mesh axis runs over, the one named last changes fastest.
Arguments:
- images: bfloat16 [32, 16, 16, 256], P('dp', 'seq'), may hold values from -6 to 6
- timesteps: int32 [32], P('dp'), may hold values from 0 to 999
- step_table: bfloat16 [1000, 512], replicated, may hold values from -6 to 6
- norm1_gain: float32 [256], replicated, may hold values from 0.1 to 1.9
- norm1_bias: float32 [256], replicated, may hold values from -3 to 3
- conv1_weight: bfloat16 [3, 3, 256, 256], replicated, may hold values from -0.125 to 0.125
- embed_weight: bfloat16 [512, 256], replicated, may hold values from -0.25 to 0.25
- embed_bias: float32 [256], replicated, may hold values from -3 to 3
- norm2_gain: float32 [256], replicated, may hold values from 0.1 to 1.9
- norm2_bias: float32 [256], replicated, may hold values from -3 to 3
- conv2_weight: bfloat16 [3, 3, 256, 256], replicated, may hold values from -0.125 to 0.125
- conv2_bias: float32 [256], replicated, may hold values from -3 to 3
- norm3_gain: float32 [256], replicated, may hold values from 0.1 to 1.9
- norm3_bias: float32 [256], replicated, may hold values from -3 to 3
- qkv_weight: bfloat16 [256, 768], replicated, may hold values from -0.5 to 0.5
- query_bias: float32 [256], replicated, may hold values from -3 to 3
- out_weight: bfloat16 [256, 256], replicated, may hold values from -1.5 to 1.5
- out_bias: float32 [256], replicated, may hold values from -3 to 3
- cotangent: bfloat16 [32, 16, 16, 256], P('dp', 'seq'), may hold values from -6 to 6
Outputs:
- output: bfloat16 [32, 16, 16, 256], P('dp', 'seq')
- grad_images: bfloat16 [32, 16, 16, 256], P('dp', 'seq')
- grad_step_table: float32 [1000, 512], replicated
- grad_norm1_gain: float32 [256], replicated
- grad_norm1_bias: float32 [256], replicated
- grad_conv1_weight: float32 [3, 3, 256, 256], replicated
- grad_embed_weight: float32 [512, 256], replicated
- grad_embed_bias: float32 [256], replicated
- grad_norm2_gain: float32 [256], replicated
- grad_norm2_bias: float32 [256], replicated
- grad_conv2_weight: float32 [3, 3, 256, 256], replicated
- grad_conv2_bias: float32 [256], replicated
- grad_norm3_gain: float32 [256], replicated
- grad_norm3_bias: float32 [256], replicated
- grad_qkv_weight: float32 [256, 768], replicated
- grad_query_bias: float32 [256], replicated
- grad_out_weight: float32 [256, 256], replicated
- grad_out_bias: float32 [256], replicated
The draws below stay inside these ranges and needn't reach their ends.
All inputs are finite; a program needn't handle non-finite values.
Results may differ from the reference program's by a relative error of at most 0.019.
The reference program's roundings to bfloat16 on the way count: a program that leaves them out, or rounds other values in their place, can miss the bound.
Values may be sent and summed in bfloat16 or wider, within the bound.
No kernel may reach another device: no remote copies, remote signals or barrier semaphores. Data moves between devices by JAX's collectives and lax.ppermute only.
A program may use at most 64 MiB of HBM per device.

```python
import jax
import jax.numpy as jnp
from jax import lax

CHANNEL_COUNT = 256
TEMB = 512
STEPS = 1000
GROUPS = 32
H = 16
W = 16
MAPS = 32


def set_ends(array, key, low, high):
    place = [jax.random.randint(jax.random.fold_in(key, axis), (), 0, length) for axis, length in enumerate(array.shape)]
    main_axis = array.shape.index(max(array.shape))
    beside = place[:main_axis] + [(place[main_axis] + 1) % array.shape[main_axis]] + place[main_axis + 1:]
    return array.at[tuple(place)].set(low).at[tuple(beside)].set(high)


def steps_of(key, dims, split, smallest, high):
    gain = 1.0
    for axis_at, blocks in split:
        draws = jax.random.uniform(jax.random.fold_in(jax.random.fold_in(key, 6), axis_at), (blocks,), jnp.float32, smallest / len(split), high / len(split))
        gain = gain * jnp.repeat(jnp.exp(draws), dims[axis_at] // blocks).reshape((-1,) + (1,) * (len(dims) - 1 - axis_at))
    return gain


def scatter_about(rng, dims, width, bound, cuts=(), held_as=jnp.bfloat16):
    array = jax.random.normal(rng, dims, jnp.float32) * width
    if len(cuts) > 0:
        array = steps_of(rng, dims, cuts, -0.22, 0.18) * array
    return jnp.clip(array, min=-bound, max=bound).astype(held_as)


def setup_inputs(seed: int = 0) -> dict:
    key_of = jax.random.split(jax.random.key(seed), 20)
    return {
        "images": scatter_about(key_of[0], (MAPS, H, W, CHANNEL_COUNT), 1.0, 6.0, ((0, 8), (1, 4))),
        "timesteps": set_ends(jax.random.randint(key_of[1], (MAPS,), 0, STEPS), jax.random.fold_in(key_of[1], 1), 0, STEPS - 1).astype(jnp.int32),
        "step_table": scatter_about(key_of[2], (STEPS, TEMB), 1.0, 6.0),
        "norm1_gain": jnp.clip(1.0 + 0.18 * jax.random.normal(key_of[3], (CHANNEL_COUNT,), jnp.float32), 0.1, 1.9),
        "norm1_bias": scatter_about(key_of[4], (CHANNEL_COUNT,), 0.5, 3.0, (), jnp.float32),
        "conv1_weight": scatter_about(key_of[5], (3, 3, CHANNEL_COUNT, CHANNEL_COUNT), (9 * CHANNEL_COUNT) ** -0.5, 0.125),
        "embed_weight": scatter_about(key_of[6], (TEMB, CHANNEL_COUNT), TEMB ** -0.5, 0.25),
        "embed_bias": scatter_about(key_of[7], (CHANNEL_COUNT,), 0.5, 3.0, (), jnp.float32),
        "norm2_gain": jnp.clip(1.0 + 0.18 * jax.random.normal(key_of[8], (CHANNEL_COUNT,), jnp.float32), 0.1, 1.9),
        "norm2_bias": scatter_about(key_of[9], (CHANNEL_COUNT,), 0.5, 3.0, (), jnp.float32),
        "conv2_weight": scatter_about(key_of[10], (3, 3, CHANNEL_COUNT, CHANNEL_COUNT), (9 * CHANNEL_COUNT) ** -0.5, 0.125),
        "conv2_bias": scatter_about(key_of[11], (CHANNEL_COUNT,), 0.5, 3.0, (), jnp.float32),
        "norm3_gain": jnp.clip(1.0 + 0.18 * jax.random.normal(key_of[12], (CHANNEL_COUNT,), jnp.float32), 0.1, 1.9),
        "norm3_bias": scatter_about(key_of[13], (CHANNEL_COUNT,), 0.5, 3.0, (), jnp.float32),
        "qkv_weight": scatter_about(key_of[14], (CHANNEL_COUNT, 3 * CHANNEL_COUNT), (CHANNEL_COUNT // 2) ** -0.5, 0.5),
        "query_bias": scatter_about(key_of[15], (CHANNEL_COUNT,), 0.5, 3.0, (), jnp.float32),
        "out_weight": scatter_about(key_of[16], (CHANNEL_COUNT, CHANNEL_COUNT), (CHANNEL_COUNT // 16) ** -0.5, 1.5),
        "out_bias": scatter_about(key_of[17], (CHANNEL_COUNT,), 0.5, 3.0, (), jnp.float32),
        "cotangent": scatter_about(key_of[18], (MAPS, H, W, CHANNEL_COUNT), 1.0, 6.0, ((0, 8), (1, 4))),
    }


highest_precision = lax.Precision.HIGHEST
norm_eps = 1e-05
block_maps = 16

@jax.custom_vjp
def low_precision(v):
    return lax.optimization_barrier(v.astype(jnp.bfloat16)).astype(jnp.float32)

@jax.custom_vjp
def low_precision_backward(v):
    return v

def low_keep(v):
    return (low_precision(v), None)

def low_pass(kept, grad):
    return (grad,)

def back_keep(v):
    return (v, None)

def back_low(kept, grad):
    return (low_precision(grad),)
low_precision.defvjp(low_keep, low_pass)
low_precision_backward.defvjp(back_keep, back_low)

def group_norm(field, norm_gain, norm_bias):
    grouped = field.reshape(field.shape[0], field.shape[1], field.shape[2], GROUPS, field.shape[3] // GROUPS)
    group_mean = lax.optimization_barrier(jnp.mean(grouped, axis=(1, 2, 4), keepdims=True))
    square = lax.optimization_barrier(jnp.mean(grouped * grouped, axis=(1, 2, 4), keepdims=True))
    scaled = (grouped - group_mean) * lax.rsqrt(square - group_mean * group_mean + norm_eps)
    return scaled.reshape(field.shape) * norm_gain + norm_bias

def convolve(field, kernel):
    return lax.conv_general_dilated(field, kernel, (1, 1), 'SAME', dimension_numbers=('NHWC', 'HWIO', 'NHWC'), precision=highest_precision)

def forward(source, table, norm1_gain, norm1_bias, conv1_weight, embed_weight, embed_bias, norm2_gain, norm2_bias, conv2_weight, conv2_bias, norm3_gain, norm3_bias, qkv_weight, query_bias, out_weight, out_bias, onehot):
    count_maps = source.shape[0]
    embedded = jnp.dot(onehot, table, precision=highest_precision)
    projected = jnp.dot(jax.nn.silu(embedded), embed_weight, precision=highest_precision) + embed_bias
    act1 = low_precision(jax.nn.silu(group_norm(source, norm1_gain, norm1_bias)))
    hidden1 = low_precision_backward(convolve(act1, conv1_weight)) + projected[:, None, None, :]
    act2 = low_precision(jax.nn.silu(group_norm(hidden1, norm2_gain, norm2_bias)))
    hidden2 = source + low_precision_backward(convolve(act2, conv2_weight)) + conv2_bias
    normed3 = low_precision(group_norm(hidden2, norm3_gain, norm3_bias)).reshape(count_maps, H * W, CHANNEL_COUNT)
    bias_row = jnp.concatenate([query_bias, jnp.zeros((2 * CHANNEL_COUNT,), jnp.float32)])
    projections = low_precision_backward(low_precision(jnp.einsum('bpc,cd->bpd', normed3, qkv_weight, precision=highest_precision) + bias_row))
    query_rows = projections[..., :CHANNEL_COUNT]
    key_rows = projections[..., CHANNEL_COUNT:2 * CHANNEL_COUNT]
    value_rows = projections[..., 2 * CHANNEL_COUNT:]
    attention_scores = low_precision_backward(jnp.einsum('ume,upe->ump', query_rows, key_rows, precision=highest_precision) * CHANNEL_COUNT ** (-0.5))
    attention_probabilities = low_precision(jax.nn.softmax(attention_scores, axis=-1))
    attended_values = low_precision_backward(low_precision(jnp.einsum('whn,wnx->whx', attention_probabilities, value_rows, precision=highest_precision)))
    attended = jnp.einsum('bpc,cd->bpd', attended_values, out_weight, precision=highest_precision) + out_bias
    return hidden2 + attended.reshape(source.shape)

def reference(images, timesteps, step_table, norm1_gain, norm1_bias, conv1_weight, embed_weight, embed_bias, norm2_gain, norm2_bias, conv2_weight, conv2_bias, norm3_gain, norm3_bias, qkv_weight, query_bias, out_weight, out_bias, cotangent):
    params = tuple((weight_arg.astype(jnp.float32) for weight_arg in (step_table, norm1_gain, norm1_bias, conv1_weight, embed_weight, embed_bias, norm2_gain, norm2_bias, conv2_weight, conv2_bias, norm3_gain, norm3_bias, qkv_weight, query_bias, out_weight, out_bias)))
    block_count = images.shape[0] // block_maps
    block_shape = (block_count, block_maps) + images.shape[1:]
    inputs = (images.reshape(block_shape), timesteps.reshape(block_count, block_maps), cotangent.reshape(block_shape))

    def one_block(running, item):
        image_block, step_block, cot_block = item
        onehot = (step_block[:, None] == jnp.arange(STEPS, dtype=jnp.int32)[None, :]).astype(jnp.float32)

        def forward_block(source, *weights):
            return forward(source, *weights, onehot)
        result, pullback = jax.vjp(forward_block, image_block.astype(jnp.float32), *params)
        grads = pullback(cot_block.astype(jnp.float32))
        running = tuple((older + newer for older, newer in zip(running, grads[1:])))
        return (running, (result.astype(jnp.bfloat16), grads[0].astype(jnp.bfloat16)))
    start = tuple((jnp.zeros_like(weight_arg) for weight_arg in params))
    totals, (outputs, grad_inputs) = lax.scan(one_block, start, inputs)
    return (outputs.reshape(images.shape), grad_inputs.reshape(images.shape), totals[0], totals[1], totals[2], totals[3], totals[4], totals[5], totals[6], totals[7], totals[8], totals[9], totals[10], totals[11], totals[12], totals[13], totals[14], totals[15])
```

```python
import functools

import jax
import jax.numpy as jnp
from jax import lax
from jax.experimental import pallas as pl
from jax.experimental.pallas import tpu as pltpu
from jax.sharding import PartitionSpec as P

GROUPS = 32
EPS = 1e-5
F32 = jnp.float32
BF16 = jnp.bfloat16
HIGHEST = lax.Precision.HIGHEST
EARLY_COST = 20 * 10**9
LONG_COST = 40 * 10**9
SUM_COST = 10**9
SMALL_COST = 10**9
UNPACK_COST = 3 * 10**8
AXES = ("dp", "seq")
VMEM = pl.BlockSpec(memory_space=pltpu.VMEM)
SMEM = pl.BlockSpec(memory_space=pltpu.SMEM)
HBM = pl.BlockSpec(memory_space=pltpu.HBM)
ANY = pl.BlockSpec(memory_space=pl.ANY)
N1_GAIN, N1_BIAS, N2_GAIN, N2_BIAS, C2_BIAS, N3_GAIN, N3_BIAS, Q_BIAS, O_BIAS, PROJECTED = range(10)
N3G, N3B, QB, OB, C2B, N2G, N2B, EB = range(8)
HIGH, LOW = 7, 8
VEC_ROWS = 16
EARLY_TAPS = 5
DIGIT = 32


def mm(a, b):
    return lax.dot_general(a, b, (((1,), (0,)), ((), ())), preferred_element_type=F32)


def mt(a, b):
    return lax.dot_general(a, b, (((1,), (1,)), ((), ())), preferred_element_type=F32)


def tm(a, b):
    return lax.dot_general(a, b, (((0,), (0,)), ((), ())), preferred_element_type=F32)


def three(v):
    hi = v.astype(BF16).astype(F32)
    mid = (v - hi).astype(BF16).astype(F32)
    return hi, mid, (v - hi) - mid


def rows_of(pieces, count, width):
    at = lax.broadcasted_iota(jnp.int32, (count, width), 0)
    out = jnp.zeros((count, width), F32)
    for i, piece in enumerate(pieces):
        out = jnp.where(at == i, piece, out)
    return out


def exact_rows(rows, matrix):
    pieces = [p for row in rows for p in three(row)]
    out = mm(rows_of(pieces, 16, rows[0].shape[1]).astype(BF16), matrix)
    return [out[3 * i : 3 * i + 1] + out[3 * i + 1 : 3 * i + 2] + out[3 * i + 2 : 3 * i + 3] for i in range(len(rows))]


def spread_matrix(c):
    per = c // GROUPS
    a = lax.broadcasted_iota(jnp.int32, (c, c), 0) // per
    b = lax.broadcasted_iota(jnp.int32, (c, c), 1) // per
    return jnp.where(a == b, 1.0, 0.0).astype(BF16)


def col_sum(v):
    return jnp.sum(v, axis=0, keepdims=True)


def norm_stats(v, spread, count):
    m, s = exact_rows([col_sum(v), col_sum(v * v)], spread)
    m = m / count
    s = s / count
    return m, lax.rsqrt(s - m * m + EPS)


def norm_back(d, hat, inv, gain, spread, count):
    bias_sum = col_sum(d)
    gain_sum = col_sum(d * hat)
    m1, m2 = exact_rows([bias_sum * gain, gain_sum * gain], spread)
    return inv * (d * gain - m1 / count - hat * (m2 / count)), gain_sum, bias_sum


def silu(v):
    return v / (1.0 + jnp.exp(-v))


def silu_slope(v):
    s = 1.0 / (1.0 + jnp.exp(-v))
    return s * (1.0 + v * (1.0 - s))


def put_shifted(ref, v, w):
    px, c = v.shape
    col = lax.broadcasted_iota(jnp.int32, (px, c), 0) % w
    edge = jnp.zeros((w, 3 * c), BF16)
    ref[0:w, :] = edge
    ref[w + px : 2 * w + px, :] = edge
    ref[w : w + px, 0:c] = jnp.where(col == 0, 0.0, pltpu.roll(v, 1, 0)).astype(BF16)
    ref[w : w + px, c : 2 * c] = v.astype(BF16)
    ref[w : w + px, 2 * c : 3 * c] = jnp.where(col == w - 1, 0.0, pltpu.roll(v, px - 1, 0)).astype(BF16)


def conv(ref, weight_ref, px, w):
    k = ref.shape[1]
    return sum(mm(ref[a * w : a * w + px, :], weight_ref[a * k : (a + 1) * k, :]) for a in range(3))


def device():
    return lax.axis_index("dp") * lax.axis_size("seq") + lax.axis_index("seq")


def digit(step):
    low, radix = step
    index = device()
    if low(0) == low(1):
        return (index >> low(0)) & (radix - 1)
    return jnp.where(index & 1 == 0, index >> low(0), index >> low(1)) & (radix - 1)


def put_halves(keep_ref, send_ref, at, v):
    n, c = v.shape
    half = c // 2
    lo = v[:, :half].astype(BF16)
    hi = v[:, half:].astype(BF16)
    first = device() & 1 == 0
    keep_ref[at : at + n, :] = jnp.where(first, lo, hi)
    send_ref[at : at + n, :] = jnp.where(first, hi, lo)


def padded(n, unit):
    return -(-n // unit) * unit


def sums_rows(total):
    return 2 * (VEC_ROWS + total)


def own_rows(total):
    return padded(32, 2 * total)


def put_both(keep_ref, send_ref, at, v):
    n, c = v.shape
    half = c // 2
    for i in range(2):
        part = v[:, i * half : (i + 1) * half].astype(BF16)
        keep_ref[at + i * n : at + (i + 1) * n, :] = part
        send_ref[at + i * n : at + (i + 1) * n, :] = part


def tap_grad(act_t, ref, tap, px, w):
    c = act_t.shape[0]
    a, b = tap // 3, tap % 3
    return mm(act_t, ref[(2 - a) * w : (2 - a) * w + px, (2 - b) * c : (3 - b) * c])


def at_rows(place, size):
    return pl.ds(pl.multiple_of(place * size, 16), size)


def pack_kernel(first_hbm, second_hbm, *refs):
    outs, sems = refs[:-1], refs[-1]
    copies = []
    for o, out in enumerate(outs):
        to = lax.axis_index("seq") ^ o
        for i, source in enumerate((first_hbm, second_hbm)):
            copies.append(pltpu.make_async_copy(source.at[to], out.at[i], sems.at[2 * o + i]))
    for copy in copies:
        copy.start()
    for copy in copies:
        copy.wait()


def unpack_kernel(*refs):
    parts, (first_ref, second_ref, token_ref) = refs[:-4], refs[-3:]
    token_ref[...] = jnp.zeros_like(token_ref)
    for o, part in enumerate(parts):
        at = lax.axis_index("seq") ^ o
        first_ref[at] = part[0]
        second_ref[at] = part[1]


def setup_kernel(steps_ref, table_ref, embed_ref, conv1_ref, conv2_ref, qkv_ref, out_ref, *refs):
    vec_refs = refs[:10]
    vec_ref, turned1_ref, turned2_ref, qkv_turned_ref, out_turned_ref = refs[10:]
    c = out_ref.shape[0]
    steps = table_ref.shape[0]
    step = steps_ref[lax.axis_index("seq")]
    pick = jnp.where(lax.broadcasted_iota(jnp.int32, (16, steps), 1) == step, 1.0, 0.0).astype(BF16)
    lifted = silu(mm(pick, table_ref[...])[0:1, :])
    (projected,) = exact_rows([lifted], embed_ref[...])
    rows = [r[...] for r in vec_refs]
    rows[PROJECTED] = rows[PROJECTED] + projected
    vec_ref[...] = rows_of(rows, 16, c)
    for source, turned in ((conv1_ref, turned1_ref), (conv2_ref, turned2_ref)):
        for tap in range(9):
            turned[(8 - tap) * c : (9 - tap) * c, :] = source[tap * c : (tap + 1) * c, :].T
    for i in range(3):
        qkv_turned_ref[i * c : (i + 1) * c, :] = qkv_ref[:, i * c : (i + 1) * c].T
    out_turned_ref[...] = out_ref[...].T


def main_kernel(w, vec_ref, conv1_ref, conv2_ref, qkv_ref, out_ref, qkv_turned_ref, out_turned_ref, *refs):
    parts, refs = refs[:-12], refs[-12:]
    (
        keep_ref, send_ref, small_ref, output_ref, image_ref, act1_ref, hat2_ref, dh2_ref, q2_ref, stat_ref,
        cot_ref, p_ref,
    ) = refs
    px, c = act1_ref.shape
    count = float(px * (c // GROUPS))
    scale = c ** (-0.5)
    spread = spread_matrix(c)
    vec = lambda i: vec_ref[i : i + 1, :]
    for o, part in enumerate(parts):
        rows = at_rows(lax.axis_index("seq") ^ o, part.shape[1])
        image_ref[rows, :] = part[0]
        cot_ref[rows, :] = part[1]

    source = image_ref[...].astype(F32)
    m1, inv1 = norm_stats(source, spread, count)
    act1 = silu((source - m1) * inv1 * vec(N1_GAIN) + vec(N1_BIAS))
    act1_ref[...] = act1.astype(BF16)
    put_shifted(p_ref, act1, w)
    hidden1 = conv(p_ref, conv1_ref, px, w) + vec(PROJECTED)
    m2, inv2 = norm_stats(hidden1, spread, count)
    hat2 = (hidden1 - m2) * inv2
    hat2_ref[...] = hat2
    stat_ref[...] = rows_of([m1, inv1, inv2], 8, c)
    act2 = silu(hat2 * vec(N2_GAIN) + vec(N2_BIAS))
    put_shifted(p_ref, act2, w)
    hidden2 = image_ref[...].astype(F32) + conv(p_ref, conv2_ref, px, w) + vec(C2_BIAS)
    act2_t = p_ref[w : w + px, c : 2 * c].T

    m3, inv3 = norm_stats(hidden2, spread, count)
    hat3 = (hidden2 - m3) * inv3
    normed3 = (hat3 * vec(N3_GAIN) + vec(N3_BIAS)).astype(BF16)
    qkv = mm(normed3, qkv_ref[...])
    q = (qkv[:, :c] + vec(Q_BIAS)).astype(BF16)
    k = qkv[:, c : 2 * c].astype(BF16)
    v = qkv[:, 2 * c :].astype(BF16)
    scores = mt(q, k) * scale
    e = jnp.exp(scores - jnp.max(scores, axis=1, keepdims=True))
    probs = e / jnp.sum(e, axis=1, keepdims=True)
    low = probs.astype(BF16)
    mixed = mm(low, v).astype(BF16)
    output_ref[...] = (hidden2 + mm(mixed, out_ref[...]) + vec(O_BIAS)).astype(BF16)

    cot = cot_ref[...]
    put_halves(keep_ref, send_ref, 12 * c, tm(mixed, cot))
    cot_wide = cot.astype(F32)
    d_mixed = mm(cot, out_turned_ref[...]).astype(BF16)
    d_probs = mt(d_mixed, v)
    inner = jnp.sum(probs * d_probs, axis=1, keepdims=True)
    d_scores = (probs * (d_probs - inner)).astype(BF16)
    d_q = (mm(d_scores, k) * scale).astype(BF16)
    d_k = (tm(d_scores, q) * scale).astype(BF16)
    d_v = tm(low, d_mixed).astype(BF16)
    normed3_t = normed3.T
    for i, d in enumerate((d_q, d_k, d_v)):
        put_halves(keep_ref, send_ref, (9 + i) * c, mm(normed3_t, d))
    d_normed3 = mm(jnp.concatenate([d_q, d_k, d_v], axis=1), qkv_turned_ref[...])
    d_src3, g_n3g, g_n3b = norm_back(d_normed3, hat3, inv3, vec(N3_GAIN), spread, count)
    d_hidden2 = cot_wide + d_src3
    dh2_ref[...] = d_hidden2
    put_shifted(q2_ref, d_hidden2, w)
    for tap in range(9):
        put_halves(keep_ref, send_ref, tap * c, tap_grad(act2_t, q2_ref, tap, px, w))
    sums = [g_n3g, g_n3b, col_sum(d_q.astype(F32)), col_sum(cot_wide), col_sum(d_hidden2)]
    small_ref[...] = rows_of(sums, 8, c)


def back_kernel(
    w, total, steps_ref, vec_ref, turned2_ref, act1_ref, hat2_ref, q2_ref, stat_ref, small_ref, keep_ref, send_ref, q1_ref,
):
    px, c = act1_ref.shape
    count = float(px * (c // GROUPS))
    spread = spread_matrix(c)
    vec = lambda i: vec_ref[i : i + 1, :]
    hat2 = hat2_ref[...]
    d = conv(q2_ref, turned2_ref, px, w) * silu_slope(hat2 * vec(N2_GAIN) + vec(N2_BIAS))
    d_hidden1, g_n2g, g_n2b = norm_back(d, hat2, stat_ref[2:3, :], vec(N2_GAIN), spread, count)
    put_shifted(q1_ref, d_hidden1, w)
    act1_t = act1_ref[...].T
    for tap in range(9):
        put_halves(keep_ref, send_ref, tap * c, tap_grad(act1_t, q1_ref, tap, px, w))

    step = steps_ref[lax.axis_index("seq")]
    lane = lax.broadcasted_iota(jnp.int32, (1, c), 1) == device()
    digits = [jnp.where(lane, d, 0).astype(F32) for d in (step // DIGIT, step % DIGIT)]
    rows = [small_ref[i : i + 1, :] for i in range(5)] + [g_n2g, g_n2b] + digits
    own = lax.broadcasted_iota(jnp.int32, (total, c), 0) == device()
    sums = [rows_of(rows, VEC_ROWS, c), jnp.where(own, col_sum(d_hidden1), 0.0)]
    put_both(keep_ref, send_ref, keep_ref.shape[0] - sums_rows(total), jnp.concatenate(sums, axis=0))


def source_kernel(
    w, vec_ref, turned1_ref, image_ref, dh2_ref, q1_ref, stat_ref, output_ref, token_ref, own_ref, *refs
):
    parts, grad_ref = refs[:-1], refs[-1]
    px, c = image_ref.shape
    count = float(px * (c // GROUPS))
    spread = spread_matrix(c)
    vec = lambda i: vec_ref[i : i + 1, :]
    inv1 = stat_ref[1:2, :]
    hat1 = (image_ref[...].astype(F32) - stat_ref[0:1, :]) * inv1
    d = conv(q1_ref, turned1_ref, px, w) * silu_slope(hat1 * vec(N1_GAIN) + vec(N1_BIAS))
    d_src1, g_n1g, g_n1b = norm_back(d, hat1, inv1, vec(N1_GAIN), spread, count)
    grad_ref[...] = (dh2_ref[...] + d_src1).astype(BF16)
    for o, part in enumerate(parts):
        rows = at_rows(lax.axis_index("seq") ^ o, part.shape[1])
        part[0] = output_ref[rows, :]
        part[1] = grad_ref[rows, :]

    half = c // 2
    own_ref[...] = jnp.zeros(own_ref.shape, BF16)
    for i in range(2):
        rows = rows_of([g_n1g[:, i * half : (i + 1) * half], g_n1b[:, i * half : (i + 1) * half]], 16, half)
        own_ref[16 * i : 16 * i + 16, :] = rows.astype(BF16)


def add_kernel(step, groups, outputs, *refs):
    count = sum(g[0] for g in groups)
    outs = refs[count + 1 :]
    radix = step[1] if step else 1
    starts = [0] * len(outs)
    used = 0
    for i, (n, first, rows, whole) in enumerate(groups):
        ins = refs[used : used + n]
        used += n
        size = rows if whole else rows // radix
        targets = range(radix) if step else [0 if i < outputs[0] else 1]
        for o in targets:
            if step and not whole:
                where = pl.ds(pl.multiple_of(first + (digit(step) ^ o) * size, 16), size)
            else:
                where = slice(first, first + size)
            total = sum(r[where, :].astype(F32) for r in ins).astype(BF16)
            outs[o][starts[o] : starts[o] + size, :] = total
            starts[o] += size


def join_kernel(step, sizes, *refs):
    ins, outs = refs[: step[1]], refs[step[1] + 1 :]
    at = 0
    for out, parts in zip(outs, sizes):
        base = 0
        for rows in parts:
            size = rows // step[1]
            for o, part in enumerate(ins):
                where = base + (digit(step) ^ o) * size
                out[pl.ds(pl.multiple_of(where, 16), size), :] = part[at : at + size, :]
            base += rows
            at += size


class Writer:
    def __init__(self, sems):
        self.sems = sems
        self.copies = []

    def send(self, source, target):
        copy = pltpu.make_async_copy(source, target, self.sems.at[len(self.copies)])
        copy.start()
        self.copies.append(copy)

    def half(self, source, at, buffer, where, target, row, col):
        n = 2 * source.shape[1]
        buffer[where : where + n, :] = source[at : at + n, :].astype(F32)
        cols = pl.ds(pl.multiple_of(col, 128), source.shape[1])
        self.send(buffer.at[pl.ds(where, n)], target.at[pl.ds(row, n), cols])

    def more(self, source, core, buffer, conv2_hbm, qkv_hbm, out_hbm):
        c = out_hbm.shape[0]
        plan = [(conv2_hbm, tap * c, 0) for tap in range(EARLY_TAPS, 9)]
        plan += [(qkv_hbm, 0, i * c) for i in range(3)] + [(out_hbm, 0, 0)]
        for i, (target, row, col) in enumerate(plan):
            self.half(source, i * c, buffer, i * c, target, row, col + core * (c // 2))

    def first(self, source, core, buffer, at, conv1_hbm):
        c = conv1_hbm.shape[1]
        for tap in range(9):
            self.half(source, tap * c, buffer, at + tap * c, conv1_hbm, tap * c, core * (c // 2))

    def wait(self):
        for copy in self.copies:
            copy.wait()


def exact_tm(a, b):
    return tm(jnp.concatenate(a, axis=0).astype(BF16), jnp.concatenate(b, axis=0).astype(BF16))


def table_kernel(total, sums_ref, table_ref, embed_ref, token_in, grad_table_hbm, grad_embed_hbm, *refs):
    vec_refs, token_ref = refs[:8], refs[8]
    grad_table_ref, grad_embed_ref, sems = refs[9:]
    token_ref[...] = jnp.zeros_like(token_ref)
    steps = table_ref.shape[0]
    writer = Writer(sems)
    n = VEC_ROWS + total

    def take(row, rows):
        return sums_ref[row : row + rows, :].astype(F32), sums_ref[n + row : n + row + rows, :].astype(F32)

    d_proj = jnp.concatenate(take(VEC_ROWS, total), axis=1)
    rows = jnp.concatenate(take(0, VEC_ROWS), axis=1)
    both = rows[HIGH : HIGH + 1, :] * DIGIT + rows[LOW : LOW + 1, :]
    c = both.shape[1]
    own = lax.broadcasted_iota(jnp.int32, (total, c), 0) == lax.broadcasted_iota(jnp.int32, (total, c), 1)
    step = jnp.sum(jnp.where(own, both, 0.0), axis=1, keepdims=True).astype(jnp.int32)
    pick = jnp.where(lax.broadcasted_iota(jnp.int32, (total, steps), 1) == step, 1.0, 0.0)
    embedded = mm(pick.astype(BF16), table_ref[...])
    d_lifted = mt(d_proj.astype(BF16), embed_ref[...])
    d_embedded = d_lifted * silu_slope(embedded)
    pieces = three(d_embedded)
    for at in range(0, steps, 256):
        part = slice(at, min(at + 256, steps))
        grad_table_ref[part, :] = exact_tm([pick[:, part]] * 3, pieces)
        writer.send(grad_table_ref.at[part], grad_table_hbm.at[part])
    grad_embed_ref[...] = exact_tm(three(silu(embedded)), [d_proj] * 3)
    writer.send(grad_embed_ref, grad_embed_hbm)
    for i, ref in enumerate(vec_refs):
        ref[...] = col_sum(d_proj) if i == EB else rows[i : i + 1, :]
    writer.wait()


def early_kernel(own, mine_ref, got_ref, token_ref, conv2_hbm, gain_ref, bias_ref, out_token_ref, conv_ref, sems):
    c = conv2_hbm.shape[1]
    half = c // 2
    out_token_ref[...] = jnp.zeros_like(out_token_ref)
    at = mine_ref.shape[0] - own
    for i in range(2):
        rows = slice(at + 16 * i, at + 16 * i + 16)
        both = mine_ref[rows, :].astype(F32) + got_ref[rows, :].astype(F32)
        gain_ref[:, i * half : (i + 1) * half] = both[0:1, :]
        bias_ref[:, i * half : (i + 1) * half] = both[1:2, :]
    first = device() & 1 == 0
    writer = Writer(sems)
    for tap in range(EARLY_TAPS):
        rows = slice(tap * c, (tap + 1) * c)
        a, b = mine_ref[rows, :].astype(F32), got_ref[rows, :].astype(F32)
        conv_ref[rows, :half] = jnp.where(first, a, b)
        conv_ref[rows, half:] = jnp.where(first, b, a)
        writer.send(conv_ref.at[rows], conv2_hbm.at[rows])
    writer.wait()


def middle_kernel(more_ref, first_ref, conv2_in, conv1_hbm, conv2_hbm, qkv_hbm, out_hbm, buffer, sems):
    writer = Writer(sems)
    core = device() & 1
    writer.more(more_ref, core, buffer, conv2_hbm, qkv_hbm, out_hbm)
    writer.first(first_ref, core, buffer, (13 - EARLY_TAPS) * out_hbm.shape[0], conv1_hbm)
    writer.wait()


def more_kernel(more_ref, conv2_in, qkv_in, out_in, token_ref, conv2_hbm, qkv_hbm, out_hbm, buffer, sems):
    writer = Writer(sems)
    writer.more(more_ref, 1 - (device() & 1), buffer, conv2_hbm, qkv_hbm, out_hbm)
    writer.wait()


def first_kernel(first_ref, conv1_in, conv1_hbm, token_ref, buffer, sems):
    token_ref[...] = jnp.zeros_like(token_ref)
    writer = Writer(sems)
    writer.first(first_ref, 1 - (device() & 1), buffer, 0, conv1_hbm)
    writer.wait()


def call(kernel, outs, specs, out_specs=None, scratch=(), limit=40, cost=1, aliases={}):
    return pl.pallas_call(
        kernel,
        out_shape=outs,
        in_specs=specs,
        out_specs=out_specs or [VMEM] * len(outs),
        scratch_shapes=scratch,
        input_output_aliases=aliases,
        compiler_params=pltpu.CompilerParams(vmem_limit_bytes=limit * 2**20),
        cost_estimate=pl.CostEstimate(flops=cost, bytes_accessed=1, transcendentals=0),
    )


def permute(array, partner, total):
    return lax.ppermute(array, AXES, [(i, partner(i)) for i in range(total)])


class Chain:
    def __init__(self, total, groups):
        self.total = total
        self.groups = groups

    def swap(self, array, low, offset):
        return permute(array, lambda i: i ^ (offset << low(i)), self.total)

    def add(self, step, token, cost=1, outputs=None):
        low, radix = step or (None, 1)
        flat = [p for g in self.groups for p in g[0]]
        sizes = [g[2] if g[3] else g[2] // radix for g in self.groups]
        outputs = outputs or [len(sizes)]
        cuts = [sum(sizes[: outputs[0]]), sum(sizes[outputs[0] :])][: len(outputs)]
        outs = [jax.ShapeDtypeStruct((n, flat[0].shape[1]), BF16) for n in (cuts if radix == 1 else cuts * radix)]
        groups = [(len(g[0]), g[1], g[2], g[3]) for g in self.groups]
        kernel = functools.partial(add_kernel, step, groups, outputs)
        outs = call(kernel, outs, [VMEM] * len(flat) + [ANY], cost=cost)(*flat, token)
        if len(outputs) > 1:
            self.parts = outs[:1]
            return outs
        self.parts = [outs[0]] + [self.swap(a, low, o + 1) for o, a in enumerate(outs[1:])]
        self.groups = [(self.parts, sum(sizes[:i]), n, g[3]) for i, (n, g) in enumerate(zip(sizes, self.groups))]
        return outs[0]

    def spread(self, step):
        low, radix = step
        self.parts = [self.parts[0]] + [self.swap(self.parts[0], low, o) for o in range(1, radix)]
        self.groups = [(self.parts,) + g[1:] for g in self.groups]

    def join(self, step, token, cost=1, sizes=None, every=False):
        rows, cols = self.parts[0].shape
        sizes = sizes or [[rows * step[1]]]
        outs = [jax.ShapeDtypeStruct((sum(n), cols), BF16) for n in sizes]
        kernel = functools.partial(join_kernel, step, sizes)
        self.parts = call(kernel, outs, [VMEM] * step[1] + [ANY], cost=cost)(*self.parts, token)
        return self.parts if every else self.parts[0]


def plan(total):
    bits = total.bit_length() - 1
    assert bits > 3 and 2**bits == total
    near = [(lambda i: 1 if i & 1 == 0 else 2, 2), (lambda i: 2 if i & 1 == 0 else 1, 2)]
    far = []
    low = 3
    while low < bits:
        take = min(2, bits - low)
        far.append((lambda i, low=low: low, 2**take))
        low += take
    return (lambda i: 0, 2), near, far


def shards(
    images, timesteps, step_table, norm1_gain, norm1_bias, conv1_weight, embed_weight, embed_bias,
    norm2_gain, norm2_bias, conv2_weight, conv2_bias, norm3_gain, norm3_bias, qkv_weight, query_bias,
    out_weight, out_bias, cotangent,
):
    maps, rows_here, w, c = images.shape
    seq = lax.axis_size("seq")
    total = lax.axis_size("dp") * seq
    assert maps == seq and total <= c
    px = rows_here * seq * w
    core, near, far = plan(total)
    shape = jax.ShapeDtypeStruct
    block = (maps, rows_here * w, c)
    pair = shape((2,) + block[1:], BF16)
    tiny = shape((8, c // 2), F32)
    field = lambda dtype: shape((px, c), dtype)
    shifted = (px + 2 * w, 3 * c)
    rows_a, rows_o, rows_v = padded(EARLY_TAPS * c, 2 * total), own_rows(total), sums_rows(total)
    rows_m, rows_1 = padded((13 - EARLY_TAPS) * c, 8 * total), padded(9 * c, 8 * total)
    conv1 = conv1_weight.reshape(9 * c, c)
    conv2 = conv2_weight.reshape(9 * c, c)

    def trade(parts):
        return [parts[0]] + [permute(p, lambda i, o=o + 1: i ^ o, total) for o, p in enumerate(parts[1:])]

    pieces = trade(
        call(pack_kernel, [pair] * seq, [HBM] * 2, None, [pltpu.SemaphoreType.DMA((2 * seq,))], 54, EARLY_COST)(
            images.reshape(block), cotangent.reshape(block)
        )
    )
    vectors = [norm1_gain, norm1_bias, norm2_gain, norm2_bias, conv2_bias, norm3_gain, norm3_bias, query_bias, out_bias, embed_bias]
    vec, turned1, turned2, qkv_turned, out_turned = call(
        setup_kernel,
        [shape((16, c), F32)] + [shape((n, c), BF16) for n in (9 * c, 9 * c, 3 * c, c)],
        [SMEM] + [VMEM] * 16,
        cost=EARLY_COST,
    )(timesteps, step_table, embed_weight, conv1, conv2, qkv_weight, out_weight, *[v.reshape(1, c) for v in vectors])
    half = lambda n: shape((n, c // 2), BF16)
    keep_e, send_e, small, output, image, act1, hat2, d_hidden2, q2, stats = call(
        functools.partial(main_kernel, w),
        [half(rows_a + rows_m)] * 2
        + [shape((8, c), F32), field(BF16), field(BF16), field(BF16), field(F32), field(F32), shape(shifted, BF16), shape((8, c), F32)],
        [VMEM] * (7 + seq),
        None,
        [pltpu.VMEM((px, c), BF16), pltpu.VMEM(shifted, BF16)],
    )(vec, conv1, conv2, qkv_weight, out_weight, qkv_turned, out_turned, *pieces)
    swap = lambda array: permute(array, lambda i: i ^ 1, total)
    got_e = swap(send_e)
    keep_1, send_1, q1 = call(
        functools.partial(back_kernel, w, total), [half(rows_1 + rows_v)] * 2 + [shape(shifted, BF16)], [SMEM] + [VMEM] * 7
    )(timesteps, vec, turned2, act1, hat2, q2, stats, small)
    got_1 = swap(send_1)
    m = Chain(total, [([keep_e, got_e], rows_a, rows_m, False)])
    token = m.add(near[0], q1)
    own, *results = call(
        functools.partial(source_kernel, w), [half(rows_o)] + [pair] * seq, [VMEM] * 7 + [ANY], None, [pltpu.VMEM((px, c), BF16)]
    )(vec, turned1, image, d_hidden2, q1, stats, output, token)
    results = trade(results)
    f = Chain(total, [([keep_1, got_1], 0, rows_1, False)])
    a = Chain(total, [([keep_e, got_e], 0, rows_a, False), ([own], 0, rows_o, False), ([keep_1, got_1], rows_1, rows_v, True)])

    far_cuts = [1]
    for _, radix in far:
        far_cuts.append(far_cuts[-1] * radix)
    sizes_a = lambda cuts: [[rows_a // cuts, rows_o // cuts]]
    sizes_b = lambda cuts: [[rows_m // cuts, rows_1 // cuts]]
    token = f.add(near[0], results[0])
    token = a.add(far[0], token)
    token = m.add(None, token, SMALL_COST)
    b = Chain(total, m.groups + f.groups)
    token = b.add(near[1], token)
    for step in far[1:] + [None]:
        token = a.add(step, token, LONG_COST)
    token = b.add(far[0], token)
    token = a.add(None, token)
    a.spread(near[0])
    for step in far[1:] + [None]:
        token = b.add(step, token, SUM_COST)
    b.spread(far[-1])
    token = a.add(None, token)
    a.spread(near[1])
    output, grad_images, token = call(unpack_kernel, [shape(block, BF16)] * 2 + [tiny], [VMEM] * seq + [ANY], cost=UNPACK_COST)(*results, token)
    for i in range(len(far))[::-1]:
        token = b.join(far[i], token, LONG_COST, sizes_b(4 * far_cuts[i]))
        b.spread(far[i - 1] if i else near[1])
    token, sums = a.add(None, token, LONG_COST, [2, 1])
    a.spread(far[-1])
    token = b.join(near[1], token, 1, sizes_b(2))
    b.spread(near[0])
    outs = [shape(step_table.shape, F32), shape(embed_weight.shape, F32)]
    grad_table, grad_embed, *vecs, token = call(
        functools.partial(table_kernel, total),
        outs + [shape((1, c), F32)] * 8 + [tiny],
        [VMEM] * 3 + [ANY],
        [HBM] * 2 + [VMEM] * 9,
        [pltpu.VMEM(o.shape, F32) for o in outs] + [pltpu.SemaphoreType.DMA((1 + -(-step_table.shape[0] // 256),))],
    )(sums, step_table, embed_weight, token)
    for i in range(len(far))[::-1]:
        token = a.join(far[i], token, LONG_COST, sizes_a(far_cuts[i]))
        a.spread(far[i - 1] if i else core)
    grads = [shape((9 * c, c), F32), shape((9 * c, c), F32), shape(qkv_weight.shape, F32), shape(out_weight.shape, F32)]
    grad_conv2, grad_norm1_gain, grad_norm1_bias, token = call(
        functools.partial(early_kernel, rows_o),
        grads[:1] + [shape((1, c), F32)] * 2 + [tiny],
        [VMEM] * 2 + [ANY],
        [HBM] + [VMEM] * 3,
        [pltpu.VMEM((EARLY_TAPS * c, c), F32), pltpu.SemaphoreType.DMA((EARLY_TAPS,))],
    )(*a.parts, token)
    more, first = b.join(near[0], token, 1, [[rows_m], [rows_1]], True)
    got_more, got_first = swap(more), swap(first)
    scratch = lambda blocks: [pltpu.VMEM((blocks * c, c // 2), F32), pltpu.SemaphoreType.DMA((blocks,))]
    count = 13 - EARLY_TAPS
    grad_conv1, *others = call(middle_kernel, grads, [VMEM] * 2 + [HBM], [HBM] * 4, scratch(count + 9), aliases={2: 1})(more, first, grad_conv2)
    grad_conv1, token = call(first_kernel, grads[:1] + [tiny], [VMEM, HBM], [HBM, VMEM], scratch(9), aliases={1: 0})(got_first, grad_conv1)
    grad_conv2, grad_qkv, grad_out = call(
        more_kernel, grads[1:], [VMEM] + [HBM] * 3 + [ANY], [HBM] * 3, scratch(count), aliases={1: 0, 2: 1, 3: 2}
    )(got_more, *others, token)
    one = lambda r: vecs[r].reshape(c)
    return (
        output.reshape(images.shape), grad_images.reshape(images.shape), grad_table, grad_norm1_gain.reshape(c), grad_norm1_bias.reshape(c),
        grad_conv1.reshape(conv1_weight.shape), grad_embed, one(EB), one(N2G), one(N2B), grad_conv2.reshape(conv2_weight.shape),
        one(C2B), one(N3G), one(N3B), grad_qkv, one(QB), grad_out, one(OB),
    )


def solution(mesh):
    field = P("dp", "seq", None, None)
    return jax.shard_map(
        shards,
        mesh=mesh,
        in_specs=(field, P("dp")) + (P(),) * 16 + (field,),
        out_specs=(field, field) + (P(),) * 16,
        check_vma=False,
    )
```

```python
import functools

import jax
import jax.numpy as jnp
from jax import lax
from jax.experimental import pallas as pl
from jax.experimental.pallas import tpu as pltpu
from jax.sharding import PartitionSpec as P

GROUPS = 32
EPS = 1e-5
F32 = jnp.float32
BF16 = jnp.bfloat16
HIGHEST = lax.Precision.HIGHEST
EARLY_COST = 20 * 10**9
LONG_COST = 40 * 10**9
SUM_COST = 10**9
SMALL_COST = 10**9
UNPACK_COST = 3 * 10**8
AXES = ("dp", "seq")
VMEM = pl.BlockSpec(memory_space=pltpu.VMEM)
SMEM = pl.BlockSpec(memory_space=pltpu.SMEM)
HBM = pl.BlockSpec(memory_space=pltpu.HBM)
ANY = pl.BlockSpec(memory_space=pl.ANY)
N1_GAIN, N1_BIAS, N2_GAIN, N2_BIAS, C2_BIAS, N3_GAIN, N3_BIAS, Q_BIAS, O_BIAS, PROJECTED = range(10)
N3G, N3B, QB, OB, C2B, N2G, N2B, EB = range(8)
HIGH, LOW = 7, 8
VEC_ROWS = 16
EARLY_TAPS = 5
DIGIT = 32


def mm(a, b):
    return lax.dot_general(a, b, (((1,), (0,)), ((), ())), preferred_element_type=F32)


def mt(a, b):
    return lax.dot_general(a, b, (((1,), (1,)), ((), ())), preferred_element_type=F32)


def tm(a, b):
    return lax.dot_general(a, b, (((0,), (0,)), ((), ())), preferred_element_type=F32)


def three(v):
    hi = v.astype(BF16).astype(F32)
    mid = (v - hi).astype(BF16).astype(F32)
    return hi, mid, (v - hi) - mid


def rows_of(pieces, count, width):
    at = lax.broadcasted_iota(jnp.int32, (count, width), 0)
    out = jnp.zeros((count, width), F32)
    for i, piece in enumerate(pieces):
        out = jnp.where(at == i, piece, out)
    return out


def exact_rows(rows, matrix):
    pieces = [p for row in rows for p in three(row)]
    out = mm(rows_of(pieces, 16, rows[0].shape[1]).astype(BF16), matrix)
    return [out[3 * i : 3 * i + 1] + out[3 * i + 1 : 3 * i + 2] + out[3 * i + 2 : 3 * i + 3] for i in range(len(rows))]


def over(index, n):
    return index >> (n.bit_length() - 1) if n & (n - 1) == 0 else index // n


def spread_matrix(c):
    per = c // GROUPS
    a = over(lax.broadcasted_iota(jnp.int32, (c, c), 0), per)
    b = over(lax.broadcasted_iota(jnp.int32, (c, c), 1), per)
    return jnp.where(a == b, 1.0, 0.0).astype(BF16)


def col_sum(v):
    return jnp.sum(v, axis=0, keepdims=True)


def norm_stats(v, spread, count):
    m, s = exact_rows([col_sum(v), col_sum(v * v)], spread)
    m = m * (1.0 / count)
    s = s * (1.0 / count)
    return m, lax.rsqrt(s - m * m + EPS)


def norm_back(d, hat, inv, gain, spread, count):
    bias_sum = col_sum(d)
    gain_sum = col_sum(d * hat)
    m1, m2 = exact_rows([bias_sum * gain, gain_sum * gain], spread)
    return d * (gain * inv) - hat * (m2 * inv * (1.0 / count)) - m1 * inv * (1.0 / count), gain_sum, bias_sum


def sigmoid(v):
    return 0.5 * jnp.tanh(0.5 * v) + 0.5


def silu(v):
    return v * sigmoid(v)


def silu_slope(v):
    s = sigmoid(v)
    return s * (1.0 + v * (1.0 - s))


def put_shifted(ref, v, w):
    px, c = v.shape
    row = lax.broadcasted_iota(jnp.int32, (px, c), 0)
    col = row & (w - 1) if w & (w - 1) == 0 else row % w
    edge = jnp.zeros((w, 3 * c), BF16)
    ref[0:w, :] = edge
    ref[w + px : 2 * w + px, :] = edge
    ref[w : w + px, 0:c] = jnp.where(col == 0, 0.0, pltpu.roll(v, 1, 0)).astype(BF16)
    ref[w : w + px, c : 2 * c] = v.astype(BF16)
    ref[w : w + px, 2 * c : 3 * c] = jnp.where(col == w - 1, 0.0, pltpu.roll(v, px - 1, 0)).astype(BF16)


def conv(ref, weight_ref, px, w):
    k = ref.shape[1]
    return sum(mm(ref[a * w : a * w + px, :], weight_ref[a * k : (a + 1) * k, :]) for a in range(3))


def conv_back(ref, weight_ref, px, w):
    c = weight_ref.shape[1]
    total = None
    for a in range(3):
        for b in range(3):
            tap = 3 * a + b
            part = mt(
                ref[(2 - a) * w : (2 - a) * w + px, (2 - b) * c : (3 - b) * c],
                weight_ref[tap * c : (tap + 1) * c, :],
            )
            total = part if total is None else total + part
    return total


def device():
    return lax.axis_index("dp") * lax.axis_size("seq") + lax.axis_index("seq")


def digit(step):
    low, radix = step
    index = device()
    if low(0) == low(1):
        return (index >> low(0)) & (radix - 1)
    return jnp.where(index & 1 == 0, index >> low(0), index >> low(1)) & (radix - 1)


def put_halves(keep_ref, send_ref, at, v):
    n, c = v.shape
    half = c // 2
    lo = v[:, :half].astype(BF16)
    hi = v[:, half:].astype(BF16)
    first = device() & 1 == 0
    keep_ref[at : at + n, :] = jnp.where(first, lo, hi)
    send_ref[at : at + n, :] = jnp.where(first, hi, lo)


def padded(n, unit):
    return -(-n // unit) * unit


def sums_rows(total):
    return VEC_ROWS + total


def own_rows(total):
    return padded(32, 2 * total)


def tap_grad(act_t, ref, tap, px, w):
    c = act_t.shape[0]
    a, b = tap // 3, tap % 3
    return mm(act_t, ref[(2 - a) * w : (2 - a) * w + px, (2 - b) * c : (3 - b) * c])


def at_rows(place, size):
    return pl.ds(pl.multiple_of(place * size, 16), size)


def pack_kernel(first_hbm, second_hbm, *refs):
    outs, sems = refs[:-1], refs[-1]
    count = len(outs) // 2
    copies = []
    for i, source in enumerate((first_hbm, second_hbm)):
        for o in range(count):
            at = i * count + o
            copies.append(pltpu.make_async_copy(source.at[lax.axis_index("seq") ^ o], outs[at], sems.at[at]))
    for copy in copies:
        copy.start()
    for copy in copies:
        copy.wait()


def unpack_kernel(*refs):
    parts, (first_ref, second_ref, token_ref) = refs[:-4], refs[-3:]
    token_ref[...] = jnp.zeros_like(token_ref)
    for o, part in enumerate(parts):
        at = lax.axis_index("seq") ^ o
        first_ref[at] = part[0]
        second_ref[at] = part[1]


def setup_kernel(steps_ref, table_ref, embed_ref, conv1_ref, conv2_ref, *refs):
    vec_refs, (vec_ref, spread_ref) = refs[:-2], refs[-2:]
    spread_ref[...] = spread_matrix(spread_ref.shape[0])
    steps = table_ref.shape[0]
    step = steps_ref[lax.axis_index("seq")]
    pick = jnp.where(lax.broadcasted_iota(jnp.int32, (16, steps), 1) == step, 1.0, 0.0).astype(BF16)
    lifted = silu(mm(pick, table_ref[...])[0:1, :])
    (projected,) = exact_rows([lifted], embed_ref[...])
    rows = [r[...] for r in vec_refs]
    rows[PROJECTED] = rows[PROJECTED] + projected
    vec_ref[...] = rows_of(rows, 16, vec_ref.shape[1])


def gather(parts, ref):
    for o, part in enumerate(parts):
        ref[at_rows(lax.axis_index("seq") ^ o, part.shape[0]), :] = part[...]


def forward_kernel(w, vec_ref, spread_ref, conv1_ref, conv2_ref, qkv_weight_ref, out_weight_ref, *refs):
    parts, refs = refs[:-11], refs[-11:]
    output_ref, image_ref, act1_ref, hat2_ref, act2_ref, hat3_ref, qkv_ref, probs_ref, mixed_ref, stat_ref, p_ref = refs
    px, c = act1_ref.shape
    count = float(px * (c // GROUPS))
    spread = spread_ref[...]
    vec = lambda i: vec_ref[i : i + 1, :]
    gather(parts, image_ref)
    source = image_ref[...].astype(F32)
    m1, inv1 = norm_stats(source, spread, count)
    act1 = silu((source - m1) * (inv1 * vec(N1_GAIN)) + vec(N1_BIAS))
    act1_ref[...] = act1.astype(BF16)
    put_shifted(p_ref, act1, w)
    hidden1 = conv(p_ref, conv1_ref, px, w) + vec(PROJECTED)
    m2, inv2 = norm_stats(hidden1, spread, count)
    hat2 = (hidden1 - m2) * inv2
    hat2_ref[...] = hat2
    act2 = silu(hat2 * vec(N2_GAIN) + vec(N2_BIAS))
    act2_ref[...] = act2.astype(BF16)
    put_shifted(p_ref, act2, w)
    hidden2 = image_ref[...].astype(F32) + conv(p_ref, conv2_ref, px, w) + vec(C2_BIAS)
    m3, inv3 = norm_stats(hidden2, spread, count)
    stat_ref[...] = rows_of([m1, inv1, inv2, inv3], 8, c)
    hat3 = (hidden2 - m3) * inv3
    hat3_ref[...] = hat3
    normed3 = (hat3 * vec(N3_GAIN) + vec(N3_BIAS)).astype(BF16)
    qkv = mm(normed3, qkv_weight_ref[...])
    q = (qkv[:, :c] + vec(Q_BIAS)).astype(BF16)
    k = qkv[:, c : 2 * c].astype(BF16)
    v = qkv[:, 2 * c :].astype(BF16)
    qkv_ref[:, :c] = q
    qkv_ref[:, c : 2 * c] = k
    qkv_ref[:, 2 * c :] = v
    scores = mt(q, k) * c ** (-0.5)
    e = jnp.exp(scores - jnp.max(scores, axis=1, keepdims=True))
    probs = e * (1.0 / jnp.sum(e, axis=1, keepdims=True))
    probs_ref[...] = probs
    mixed = mm(probs.astype(BF16), v).astype(BF16)
    mixed_ref[...] = mixed
    output_ref[...] = (hidden2 + mm(mixed, out_weight_ref[...]) + vec(O_BIAS)).astype(BF16)


def main_kernel(w, vec_ref, spread_ref, qkv_weight_ref, out_weight_ref, act2_ref, hat3_ref, qkv_ref, probs_ref, mixed_ref, stat_ref, *refs):
    parts, (keep_ref, send_ref, small_ref, dh2_ref, q2_ref, cot_ref) = refs[:-6], refs[-6:]
    px, c = act2_ref.shape
    count = float(px * (c // GROUPS))
    scale = c ** (-0.5)
    spread = spread_ref[...]
    vec = lambda i: vec_ref[i : i + 1, :]
    gather(parts, cot_ref)
    cot = cot_ref[...]
    cot_wide = cot.astype(F32)
    probs = probs_ref[...]
    q, k, v = qkv_ref[:, :c], qkv_ref[:, c : 2 * c], qkv_ref[:, 2 * c :]
    put_halves(keep_ref, send_ref, 12 * c, tm(mixed_ref[...], cot))
    d_mixed = mt(cot, out_weight_ref[...]).astype(BF16)
    d_probs = mt(d_mixed, v)
    inner = jnp.sum(probs * d_probs, axis=1, keepdims=True)
    d_scores = (probs * (d_probs - inner)).astype(BF16)
    d_q = (mm(d_scores, k) * scale).astype(BF16)
    d_k = (tm(d_scores, q) * scale).astype(BF16)
    d_v = tm(probs.astype(BF16), d_mixed).astype(BF16)
    hat3 = hat3_ref[...]
    normed3_t = (hat3 * vec(N3_GAIN) + vec(N3_BIAS)).astype(BF16).T
    d_normed3 = None
    for i, d in enumerate((d_q, d_k, d_v)):
        put_halves(keep_ref, send_ref, (9 + i) * c, mm(normed3_t, d))
        part = mt(d, qkv_weight_ref[:, i * c : (i + 1) * c])
        d_normed3 = part if d_normed3 is None else d_normed3 + part
    d_src3, g_n3g, g_n3b = norm_back(d_normed3, hat3, stat_ref[3:4, :], vec(N3_GAIN), spread, count)
    d_hidden2 = cot_wide + d_src3
    dh2_ref[...] = d_hidden2
    put_shifted(q2_ref, d_hidden2, w)
    act2_t = act2_ref[...].T
    for tap in range(9):
        put_halves(keep_ref, send_ref, tap * c, tap_grad(act2_t, q2_ref, tap, px, w))
    sums = [g_n3g, g_n3b, col_sum(d_q.astype(F32)), col_sum(cot_wide), col_sum(d_hidden2)]
    small_ref[...] = rows_of(sums, 8, c)


def back_kernel(
    w, total, steps_ref, vec_ref, spread_ref, conv2_ref, act1_ref, hat2_ref, q2_ref, stat_ref, small_ref, keep_ref, send_ref, q1_ref,
):
    px, c = act1_ref.shape
    count = float(px * (c // GROUPS))
    spread = spread_ref[...]
    vec = lambda i: vec_ref[i : i + 1, :]
    hat2 = hat2_ref[...]
    d = conv_back(q2_ref, conv2_ref, px, w) * silu_slope(hat2 * vec(N2_GAIN) + vec(N2_BIAS))
    d_hidden1, g_n2g, g_n2b = norm_back(d, hat2, stat_ref[2:3, :], vec(N2_GAIN), spread, count)
    put_shifted(q1_ref, d_hidden1, w)
    act1_t = act1_ref[...].T
    for tap in range(9):
        put_halves(keep_ref, send_ref, tap * c, tap_grad(act1_t, q1_ref, tap, px, w))

    step = steps_ref[lax.axis_index("seq")]
    lane = lax.broadcasted_iota(jnp.int32, (1, c), 1) == device()
    digits = [jnp.where(lane, d, 0).astype(F32) for d in (step // DIGIT, step % DIGIT)]
    rows = [small_ref[i : i + 1, :] for i in range(5)] + [g_n2g, g_n2b] + digits
    own = lax.broadcasted_iota(jnp.int32, (total, c), 0) == device()
    sums = [rows_of(rows, VEC_ROWS, c), jnp.where(own, col_sum(d_hidden1), 0.0)]
    put_halves(keep_ref, send_ref, keep_ref.shape[0] - sums_rows(total), jnp.concatenate(sums, axis=0))


def source_kernel(
    w, vec_ref, spread_ref, conv1_ref, image_ref, dh2_ref, q1_ref, stat_ref, output_ref, token_ref, own_ref, *refs
):
    parts, grad_ref = refs[:-1], refs[-1]
    px, c = image_ref.shape
    count = float(px * (c // GROUPS))
    spread = spread_ref[...]
    vec = lambda i: vec_ref[i : i + 1, :]
    inv1 = stat_ref[1:2, :]
    hat1 = (image_ref[...].astype(F32) - stat_ref[0:1, :]) * inv1
    d = conv_back(q1_ref, conv1_ref, px, w) * silu_slope(hat1 * vec(N1_GAIN) + vec(N1_BIAS))
    d_src1, g_n1g, g_n1b = norm_back(d, hat1, inv1, vec(N1_GAIN), spread, count)
    grad_ref[...] = (dh2_ref[...] + d_src1).astype(BF16)
    for o, part in enumerate(parts):
        rows = at_rows(lax.axis_index("seq") ^ o, part.shape[1])
        part[0] = output_ref[rows, :]
        part[1] = grad_ref[rows, :]

    half = c // 2
    own_ref[...] = jnp.zeros(own_ref.shape, BF16)
    for i in range(2):
        rows = rows_of([g_n1g[:, i * half : (i + 1) * half], g_n1b[:, i * half : (i + 1) * half]], 16, half)
        own_ref[16 * i : 16 * i + 16, :] = rows.astype(BF16)


def add_kernel(step, groups, outputs, *refs):
    count = sum(g[0] for g in groups)
    outs = refs[count + 1 :]
    radix = step[1] if step else 1
    starts = [0] * len(outs)
    used = 0
    for i, (n, first, rows, whole) in enumerate(groups):
        ins = refs[used : used + n]
        used += n
        size = rows if whole else rows // radix
        targets = range(radix) if step else [0 if i < outputs[0] else 1]
        for o in targets:
            if step and not whole:
                where = pl.ds(pl.multiple_of(first + (digit(step) ^ o) * size, 16), size)
            else:
                where = slice(first, first + size)
            total = sum(r[where, :].astype(F32) for r in ins).astype(BF16)
            outs[o][starts[o] : starts[o] + size, :] = total
            starts[o] += size


def join_kernel(step, sizes, *refs):
    ins, outs = refs[: step[1]], refs[step[1] + 1 :]
    at = 0
    for out, parts in zip(outs, sizes):
        base = 0
        for rows in parts:
            size = rows // step[1]
            for o, part in enumerate(ins):
                where = base + (digit(step) ^ o) * size
                out[pl.ds(pl.multiple_of(where, 16), size), :] = part[at : at + size, :]
            base += rows
            at += size


class Writer:
    def __init__(self, sems):
        self.sems = sems
        self.copies = []

    def send(self, source, target):
        copy = pltpu.make_async_copy(source, target, self.sems.at[len(self.copies)])
        copy.start()
        self.copies.append(copy)

    def half(self, source, at, buffer, where, target, row, col):
        n = 2 * source.shape[1]
        buffer[where : where + n, :] = source[at : at + n, :].astype(F32)
        cols = pl.ds(pl.multiple_of(col, 128), source.shape[1])
        self.send(buffer.at[pl.ds(where, n)], target.at[pl.ds(row, n), cols])

    def more(self, source, core, buffer, conv2_hbm, qkv_hbm, out_hbm):
        c = out_hbm.shape[0]
        plan = [(conv2_hbm, tap * c, 0) for tap in range(EARLY_TAPS, 9)]
        plan += [(qkv_hbm, 0, i * c) for i in range(3)] + [(out_hbm, 0, 0)]
        for i, (target, row, col) in enumerate(plan):
            self.half(source, i * c, buffer, i * c, target, row, col + core * (c // 2))

    def first(self, source, start, core, buffer, at, conv1_hbm):
        c = conv1_hbm.shape[1]
        for tap in range(9):
            self.half(source, start + tap * c, buffer, at + tap * c, conv1_hbm, tap * c, core * (c // 2))

    def wait(self):
        for copy in self.copies:
            copy.wait()


def exact_tm(a, b):
    return tm(jnp.concatenate(a, axis=0).astype(BF16), jnp.concatenate(b, axis=0).astype(BF16))


def table_kernel(total, sums_ref, got_ref, table_ref, embed_ref, token_in, grad_table_hbm, grad_embed_hbm, *refs):
    vec_refs, token_ref = refs[:8], refs[8]
    grad_table_ref, grad_embed_ref, sems = refs[9:]
    token_ref[...] = jnp.zeros_like(token_ref)
    steps = table_ref.shape[0]
    writer = Writer(sems)
    left = device() & 1 == 0

    def take(row, rows):
        a, b = [ref[row : row + rows, :].astype(F32) for ref in (sums_ref, got_ref)]
        return jnp.where(left, a, b), jnp.where(left, b, a)

    d_proj = jnp.concatenate(take(VEC_ROWS, total), axis=1)
    rows = jnp.concatenate(take(0, VEC_ROWS), axis=1)
    both = rows[HIGH : HIGH + 1, :] * DIGIT + rows[LOW : LOW + 1, :]
    c = both.shape[1]
    own = lax.broadcasted_iota(jnp.int32, (total, c), 0) == lax.broadcasted_iota(jnp.int32, (total, c), 1)
    step = jnp.sum(jnp.where(own, both, 0.0), axis=1, keepdims=True).astype(jnp.int32)
    pick = jnp.where(lax.broadcasted_iota(jnp.int32, (total, steps), 1) == step, 1.0, 0.0)
    embedded = mm(pick.astype(BF16), table_ref[...])
    d_lifted = mt(d_proj.astype(BF16), embed_ref[...])
    d_embedded = d_lifted * silu_slope(embedded)
    pieces = three(d_embedded)
    for at in range(0, steps, 256):
        part = slice(at, min(at + 256, steps))
        grad_table_ref[part, :] = exact_tm([pick[:, part]] * 3, pieces)
        writer.send(grad_table_ref.at[part], grad_table_hbm.at[part])
    grad_embed_ref[...] = exact_tm(three(silu(embedded)), [d_proj] * 3)
    writer.send(grad_embed_ref, grad_embed_hbm)
    for i, ref in enumerate(vec_refs):
        ref[...] = col_sum(d_proj) if i == EB else rows[i : i + 1, :]
    writer.wait()


def early_kernel(own, mine_ref, got_ref, token_ref, conv2_hbm, gain_ref, bias_ref, out_token_ref, conv_ref, sems):
    c = conv2_hbm.shape[1]
    half = c // 2
    out_token_ref[...] = jnp.zeros_like(out_token_ref)
    at = mine_ref.shape[0] - own
    for i in range(2):
        rows = slice(at + 16 * i, at + 16 * i + 16)
        both = mine_ref[rows, :].astype(F32) + got_ref[rows, :].astype(F32)
        gain_ref[:, i * half : (i + 1) * half] = both[0:1, :]
        bias_ref[:, i * half : (i + 1) * half] = both[1:2, :]
    first = device() & 1 == 0
    writer = Writer(sems)
    for tap in range(EARLY_TAPS):
        rows = slice(tap * c, (tap + 1) * c)
        a, b = mine_ref[rows, :].astype(F32), got_ref[rows, :].astype(F32)
        conv_ref[rows, :half] = jnp.where(first, a, b)
        conv_ref[rows, half:] = jnp.where(first, b, a)
        writer.send(conv_ref.at[rows], conv2_hbm.at[rows])
    writer.wait()


def write_late(split, late_ref, core, buffer, sems, conv1_hbm, conv2_hbm, qkv_hbm, out_hbm):
    writer = Writer(sems)
    writer.more(late_ref, core, buffer, conv2_hbm, qkv_hbm, out_hbm)
    writer.first(late_ref, split, core, buffer, (13 - EARLY_TAPS) * out_hbm.shape[0], conv1_hbm)
    writer.wait()


def middle_kernel(split, late_ref, conv2_in, conv1_hbm, conv2_hbm, qkv_hbm, out_hbm, buffer, sems):
    write_late(split, late_ref, device() & 1, buffer, sems, conv1_hbm, conv2_hbm, qkv_hbm, out_hbm)


def last_kernel(split, late_ref, conv1_in, conv2_in, qkv_in, out_in, conv1_hbm, conv2_hbm, qkv_hbm, out_hbm, buffer, sems):
    write_late(split, late_ref, 1 - (device() & 1), buffer, sems, conv1_hbm, conv2_hbm, qkv_hbm, out_hbm)


def call(kernel, outs, specs, out_specs=None, scratch=(), limit=40, cost=1, aliases={}):
    return pl.pallas_call(
        kernel,
        out_shape=outs,
        in_specs=specs,
        out_specs=out_specs or [VMEM] * len(outs),
        scratch_shapes=scratch,
        input_output_aliases=aliases,
        compiler_params=pltpu.CompilerParams(vmem_limit_bytes=limit * 2**20),
        cost_estimate=pl.CostEstimate(flops=cost, bytes_accessed=1, transcendentals=0),
    )


def permute(array, partner, total):
    return lax.ppermute(array, AXES, [(i, partner(i)) for i in range(total)])


class Chain:
    def __init__(self, total, groups):
        self.total = total
        self.groups = groups

    def swap(self, array, low, offset):
        return permute(array, lambda i: i ^ (offset << low(i)), self.total)

    def add(self, step, token, cost=1, outputs=None):
        low, radix = step or (None, 1)
        flat = [p for g in self.groups for p in g[0]]
        sizes = [g[2] if g[3] else g[2] // radix for g in self.groups]
        outputs = outputs or [len(sizes)]
        cuts = [sum(sizes[: outputs[0]]), sum(sizes[outputs[0] :])][: len(outputs)]
        outs = [jax.ShapeDtypeStruct((n, flat[0].shape[1]), BF16) for n in (cuts if radix == 1 else cuts * radix)]
        groups = [(len(g[0]), g[1], g[2], g[3]) for g in self.groups]
        kernel = functools.partial(add_kernel, step, groups, outputs)
        outs = call(kernel, outs, [VMEM] * len(flat) + [ANY], cost=cost)(*flat, token)
        if len(outputs) > 1:
            self.parts = outs[:1]
            return outs
        self.parts = [outs[0]] + [self.swap(a, low, o + 1) for o, a in enumerate(outs[1:])]
        self.groups = [(self.parts, sum(sizes[:i]), n, g[3]) for i, (n, g) in enumerate(zip(sizes, self.groups))]
        return outs[0]

    def spread(self, step):
        low, radix = step
        self.parts = [self.parts[0]] + [self.swap(self.parts[0], low, o) for o in range(1, radix)]
        self.groups = [(self.parts,) + g[1:] for g in self.groups]

    def join(self, step, token, cost=1, sizes=None, every=False):
        rows, cols = self.parts[0].shape
        sizes = sizes or [[rows * step[1]]]
        outs = [jax.ShapeDtypeStruct((sum(n), cols), BF16) for n in sizes]
        kernel = functools.partial(join_kernel, step, sizes)
        self.parts = call(kernel, outs, [VMEM] * step[1] + [ANY], cost=cost)(*self.parts, token)
        return self.parts if every else self.parts[0]


def plan(total):
    bits = total.bit_length() - 1
    assert bits > 3 and 2**bits == total
    near = [(lambda i: 1 if i & 1 == 0 else 2, 2), (lambda i: 2 if i & 1 == 0 else 1, 2)]
    far = []
    low = 3
    while low < bits:
        take = min(2, bits - low)
        far.append((lambda i, low=low: low, 2**take))
        low += take
    return (lambda i: 0, 2), near, far


def shards(
    images, timesteps, step_table, norm1_gain, norm1_bias, conv1_weight, embed_weight, embed_bias,
    norm2_gain, norm2_bias, conv2_weight, conv2_bias, norm3_gain, norm3_bias, qkv_weight, query_bias,
    out_weight, out_bias, cotangent,
):
    maps, rows_here, w, c = images.shape
    seq = lax.axis_size("seq")
    total = lax.axis_size("dp") * seq
    assert maps == seq and total <= c
    px = rows_here * seq * w
    core, near, far = plan(total)
    shape = jax.ShapeDtypeStruct
    block = (maps, rows_here * w, c)
    pair = shape((2,) + block[1:], BF16)
    tiny = shape((8, c // 2), F32)
    field = lambda dtype: shape((px, c), dtype)
    shifted = (px + 2 * w, 3 * c)
    rows_a, rows_o, rows_v = padded(EARLY_TAPS * c, 2 * total), own_rows(total), sums_rows(total)
    rows_m, rows_1 = padded((13 - EARLY_TAPS) * c, 8 * total), padded(9 * c, 8 * total)
    conv1 = conv1_weight.reshape(9 * c, c)
    conv2 = conv2_weight.reshape(9 * c, c)

    def trade(parts):
        return [parts[0]] + [permute(p, lambda i, o=o + 1: i ^ o, total) for o, p in enumerate(parts[1:])]

    pieces = call(pack_kernel, [shape(block[1:], BF16)] * (2 * seq), [HBM] * 2, None, [pltpu.SemaphoreType.DMA((2 * seq,))], 54, EARLY_COST)(
        images.reshape(block), cotangent.reshape(block)
    )
    images_here, cots_here = trade(pieces[:seq]), trade(pieces[seq:])
    vectors = [norm1_gain, norm1_bias, norm2_gain, norm2_bias, conv2_bias, norm3_gain, norm3_bias, query_bias, out_bias, embed_bias]
    vec, spread = call(setup_kernel, [shape((16, c), F32), shape((c, c), BF16)], [SMEM] + [VMEM] * 2 + [ANY] * 2 + [VMEM] * 10, cost=EARLY_COST)(
        timesteps, step_table, embed_weight, conv1, conv2, *[v.reshape(1, c) for v in vectors]
    )
    half = lambda n: shape((n, c // 2), BF16)
    output, image, act1, hat2, *kept, stats = call(
        functools.partial(forward_kernel, w),
        [field(BF16), field(BF16), field(BF16), field(F32), field(BF16), field(F32), shape((px, 3 * c), BF16), field(F32), field(BF16)]
        + [shape((8, c), F32)],
        [VMEM] * (6 + seq),
        None,
        [pltpu.VMEM(shifted, BF16)],
    )(vec, spread, conv1, conv2, qkv_weight, out_weight, *images_here)
    keep_e, send_e, small, d_hidden2, q2 = call(
        functools.partial(main_kernel, w),
        [half(rows_a + rows_m)] * 2 + [shape((8, c), F32), field(F32), shape(shifted, BF16)],
        [VMEM] * (10 + seq),
        None,
        [pltpu.VMEM((px, c), BF16)],
    )(vec, spread, qkv_weight, out_weight, *kept, stats, *cots_here)
    swap = lambda array: permute(array, lambda i: i ^ 1, total)
    got_e = swap(send_e)
    keep_1, send_1, q1 = call(
        functools.partial(back_kernel, w, total), [half(rows_1 + rows_v)] * 2 + [shape(shifted, BF16)], [SMEM] + [VMEM] * 8
    )(timesteps, vec, spread, conv2, act1, hat2, q2, stats, small)
    got_1 = swap(send_1)
    m = Chain(total, [([keep_e, got_e], rows_a, rows_m, False)])
    token = m.add(near[0], q1)
    own, *results = call(
        functools.partial(source_kernel, w), [half(rows_o)] + [pair] * seq, [VMEM] * 8 + [ANY], None, [pltpu.VMEM((px, c), BF16)]
    )(vec, spread, conv1, image, d_hidden2, q1, stats, output, token)
    results = trade(results)
    f = Chain(total, [([keep_1, got_1], 0, rows_1, False)])
    a = Chain(total, [([keep_e, got_e], 0, rows_a, False), ([own], 0, rows_o, False), ([keep_1, got_1], rows_1, rows_v, True)])

    far_cuts = [1]
    for _, radix in far:
        far_cuts.append(far_cuts[-1] * radix)
    sizes_a = lambda cuts: [[rows_a // cuts, rows_o // cuts]]
    sizes_b = lambda cuts: [[rows_m // cuts, rows_1 // cuts]]
    token = f.add(near[0], results[0])
    token = a.add(far[0], token)
    token = m.add(None, token, SMALL_COST)
    b = Chain(total, m.groups + f.groups)
    token = b.add(near[1], token)
    for step in far[1:] + [None]:
        token = a.add(step, token, LONG_COST)
    token = b.add(far[0], token)
    token = a.add(None, token)
    a.spread(near[0])
    for step in far[1:] + [None]:
        token = b.add(step, token, SUM_COST)
    b.spread(far[-1])
    token = a.add(None, token)
    a.spread(near[1])
    output, grad_images, token = call(unpack_kernel, [shape(block, BF16)] * 2 + [tiny], [VMEM] * seq + [ANY], cost=UNPACK_COST)(*results, token)
    for i in range(len(far))[::-1]:
        token = b.join(far[i], token, LONG_COST, sizes_b(4 * far_cuts[i]))
        b.spread(far[i - 1] if i else near[1])
    token, sums = a.add(None, token, LONG_COST, [2, 1])
    a.spread(far[-1])
    token = b.join(near[1], token, 1, sizes_b(2))
    b.spread(near[0])
    outs = [shape(step_table.shape, F32), shape(embed_weight.shape, F32)]
    grad_table, grad_embed, *vecs, token = call(
        functools.partial(table_kernel, total),
        outs + [shape((1, c), F32)] * 8 + [tiny],
        [VMEM] * 4 + [ANY],
        [HBM] * 2 + [VMEM] * 9,
        [pltpu.VMEM(o.shape, F32) for o in outs] + [pltpu.SemaphoreType.DMA((1 + -(-step_table.shape[0] // 256),))],
    )(sums, swap(sums), step_table, embed_weight, token)
    for i in range(len(far))[::-1]:
        token = a.join(far[i], token, LONG_COST, sizes_a(far_cuts[i]))
        a.spread(far[i - 1] if i else core)
    grads = [shape((9 * c, c), F32), shape((9 * c, c), F32), shape(qkv_weight.shape, F32), shape(out_weight.shape, F32)]
    grad_conv2, grad_norm1_gain, grad_norm1_bias, token = call(
        functools.partial(early_kernel, rows_o),
        grads[:1] + [shape((1, c), F32)] * 2 + [tiny],
        [VMEM] * 2 + [ANY],
        [HBM] + [VMEM] * 3,
        [pltpu.VMEM((EARLY_TAPS * c, c), F32), pltpu.SemaphoreType.DMA((EARLY_TAPS,))],
    )(*a.parts, token)
    late = b.join(near[0], token, 1, sizes_b(1))
    got_late = swap(late)
    scratch = lambda blocks: [pltpu.VMEM((blocks * c, c // 2), F32), pltpu.SemaphoreType.DMA((blocks,))]
    count = 13 - EARLY_TAPS
    grads_half = call(
        functools.partial(middle_kernel, rows_m), grads, [VMEM] + [HBM], [HBM] * 4, scratch(count + 9), aliases={1: 1}
    )(late, grad_conv2)
    grad_conv1, grad_conv2, grad_qkv, grad_out = call(
        functools.partial(last_kernel, rows_m), grads, [VMEM] + [HBM] * 4, [HBM] * 4, scratch(count + 9), aliases={1: 0, 2: 1, 3: 2, 4: 3}
    )(got_late, *grads_half)
    one = lambda r: vecs[r].reshape(c)
    return (
        output.reshape(images.shape), grad_images.reshape(images.shape), grad_table, grad_norm1_gain.reshape(c), grad_norm1_bias.reshape(c),
        grad_conv1.reshape(conv1_weight.shape), grad_embed, one(EB), one(N2G), one(N2B), grad_conv2.reshape(conv2_weight.shape),
        one(C2B), one(N3G), one(N3B), grad_qkv, one(QB), grad_out, one(OB),
    )


def solution(mesh):
    field = P("dp", "seq", None, None)
    return jax.shard_map(
        shards,
        mesh=mesh,
        in_specs=(field, P("dp")) + (P(),) * 16 + (field,),
        out_specs=(field, field) + (P(),) * 16,
        check_vma=False,
    )
```

```python
import functools

import jax
import jax.numpy as jnp
from jax import lax
from jax.experimental import pallas as pl
from jax.experimental.pallas import tpu as pltpu
from jax.sharding import PartitionSpec as P

GROUPS = 32
EPS = 1e-5
F32 = jnp.float32
BF16 = jnp.bfloat16
HIGHEST = lax.Precision.HIGHEST
EARLY_COST = 20 * 10**9
LONG_COST = 40 * 10**9
SUM_COST = 10**9
SMALL_COST = 10**9
UNPACK_COST = 3 * 10**8
AXES = ("dp", "seq")
VMEM = pl.BlockSpec(memory_space=pltpu.VMEM)
SMEM = pl.BlockSpec(memory_space=pltpu.SMEM)
HBM = pl.BlockSpec(memory_space=pltpu.HBM)
ANY = pl.BlockSpec(memory_space=pl.ANY)
N1_GAIN, N1_BIAS, N2_GAIN, N2_BIAS, C2_BIAS, N3_GAIN, N3_BIAS, Q_BIAS, O_BIAS, PROJECTED = range(10)
N3G, N3B, QB, OB, C2B, N2G, N2B, EB = range(8)
HIGH, LOW = 7, 8
VEC_ROWS = 16
EARLY_TAPS = 6
DIGIT = 32


def mm(a, b):
    return lax.dot_general(a, b, (((1,), (0,)), ((), ())), preferred_element_type=F32)


def mt(a, b):
    return lax.dot_general(a, b, (((1,), (1,)), ((), ())), preferred_element_type=F32)


def tm(a, b):
    return lax.dot_general(a, b, (((0,), (0,)), ((), ())), preferred_element_type=F32)


def three(v):
    hi = v.astype(BF16).astype(F32)
    mid = (v - hi).astype(BF16).astype(F32)
    return hi, mid, (v - hi) - mid


def rows_of(pieces, count, width):
    at = lax.broadcasted_iota(jnp.int32, (count, width), 0)
    out = jnp.zeros((count, width), F32)
    for i, piece in enumerate(pieces):
        out = jnp.where(at == i, piece, out)
    return out


def exact_rows(rows, matrix):
    pieces = [p for row in rows for p in three(row)]
    out = mm(rows_of(pieces, 16, rows[0].shape[1]).astype(BF16), matrix)
    return [out[3 * i : 3 * i + 1] + out[3 * i + 1 : 3 * i + 2] + out[3 * i + 2 : 3 * i + 3] for i in range(len(rows))]


def over(index, n):
    return index >> (n.bit_length() - 1) if n & (n - 1) == 0 else index // n


def spread_matrix(c):
    per = c // GROUPS
    a = over(lax.broadcasted_iota(jnp.int32, (c, c), 0), per)
    b = over(lax.broadcasted_iota(jnp.int32, (c, c), 1), per)
    return jnp.where(a == b, 1.0, 0.0).astype(BF16)


def col_sum(v):
    return jnp.sum(v, axis=0, keepdims=True)


def norm_stats(v, spread, count):
    m, s = exact_rows([col_sum(v), col_sum(v * v)], spread)
    m = m * (1.0 / count)
    s = s * (1.0 / count)
    return m, lax.rsqrt(s - m * m + EPS)


def norm_back(d, hat, inv, gain, spread, count):
    bias_sum = col_sum(d)
    gain_sum = col_sum(d * hat)
    m1, m2 = exact_rows([bias_sum * gain, gain_sum * gain], spread)
    return d * (gain * inv) - hat * (m2 * inv * (1.0 / count)) - m1 * inv * (1.0 / count), gain_sum, bias_sum


def sigmoid(v):
    return 0.5 * jnp.tanh(0.5 * v) + 0.5


def silu(v):
    return v * sigmoid(v)


def silu_slope(v):
    s = sigmoid(v)
    return s * (1.0 + v * (1.0 - s))


def put_shifted(ref, v, w):
    px, c = v.shape
    row = lax.broadcasted_iota(jnp.int32, (px, c), 0)
    col = row & (w - 1) if w & (w - 1) == 0 else row % w
    edge = jnp.zeros((w, 3 * c), BF16)
    ref[0:w, :] = edge
    ref[w + px : 2 * w + px, :] = edge
    ref[w : w + px, 0:c] = jnp.where(col == 0, 0.0, pltpu.roll(v, 1, 0)).astype(BF16)
    ref[w : w + px, c : 2 * c] = v.astype(BF16)
    ref[w : w + px, 2 * c : 3 * c] = jnp.where(col == w - 1, 0.0, pltpu.roll(v, px - 1, 0)).astype(BF16)


def conv(ref, weight_ref, px, w):
    k = ref.shape[1]
    return sum(mm(ref[a * w : a * w + px, :], weight_ref[a * k : (a + 1) * k, :]) for a in range(3))


def conv_back(ref, weight_ref, px, w):
    c = weight_ref.shape[1]
    total = None
    for a in range(3):
        for b in range(3):
            tap = 3 * a + b
            part = mt(
                ref[(2 - a) * w : (2 - a) * w + px, (2 - b) * c : (3 - b) * c],
                weight_ref[tap * c : (tap + 1) * c, :],
            )
            total = part if total is None else total + part
    return total


def device():
    return lax.axis_index("dp") * lax.axis_size("seq") + lax.axis_index("seq")


def digit(step):
    low, radix = step
    index = device()
    if low(0) == low(1):
        return (index >> low(0)) & (radix - 1)
    return jnp.where(index & 1 == 0, index >> low(0), index >> low(1)) & (radix - 1)


def put_halves(keep_ref, send_ref, at, v):
    n, c = v.shape
    half = c // 2
    lo = v[:, :half].astype(BF16)
    hi = v[:, half:].astype(BF16)
    first = device() & 1 == 0
    keep_ref[at : at + n, :] = jnp.where(first, lo, hi)
    send_ref[at : at + n, :] = jnp.where(first, hi, lo)


def padded(n, unit):
    return -(-n // unit) * unit


def sums_rows(total):
    return VEC_ROWS + total


def own_rows(total):
    return padded(32, 2 * total)


def tap_grad(act_t, ref, tap, px, w):
    c = act_t.shape[0]
    a, b = tap // 3, tap % 3
    return mm(act_t, ref[(2 - a) * w : (2 - a) * w + px, (2 - b) * c : (3 - b) * c])


def at_rows(place, size):
    return pl.ds(pl.multiple_of(place * size, 16), size)


def pack_kernel(first_hbm, second_hbm, *refs):
    outs, sems = refs[:-1], refs[-1]
    count = len(outs) // 2
    copies = []
    for i, source in enumerate((first_hbm, second_hbm)):
        for o in range(count):
            at = i * count + o
            copies.append(pltpu.make_async_copy(source.at[lax.axis_index("seq") ^ o], outs[at], sems.at[at]))
    for copy in copies:
        copy.start()
    for copy in copies:
        copy.wait()


def unpack_kernel(*refs):
    parts, (first_ref, second_ref, token_ref) = refs[:-4], refs[-3:]
    token_ref[...] = jnp.zeros_like(token_ref)
    for o, part in enumerate(parts):
        at = lax.axis_index("seq") ^ o
        first_ref[at] = part[0]
        second_ref[at] = part[1]


def setup_kernel(steps_ref, table_ref, embed_ref, conv1_ref, conv2_ref, *refs):
    vec_refs, (vec_ref, spread_ref) = refs[:-2], refs[-2:]
    spread_ref[...] = spread_matrix(spread_ref.shape[0])
    steps = table_ref.shape[0]
    step = steps_ref[lax.axis_index("seq")]
    pick = jnp.where(lax.broadcasted_iota(jnp.int32, (16, steps), 1) == step, 1.0, 0.0).astype(BF16)
    lifted = silu(mm(pick, table_ref[...])[0:1, :])
    (projected,) = exact_rows([lifted], embed_ref[...])
    rows = [r[...] for r in vec_refs]
    rows[PROJECTED] = rows[PROJECTED] + projected
    vec_ref[...] = rows_of(rows, 16, vec_ref.shape[1])


def gather(parts, ref):
    for o, part in enumerate(parts):
        ref[at_rows(lax.axis_index("seq") ^ o, part.shape[0]), :] = part[...]


def forward_kernel(w, vec_ref, spread_ref, conv1_ref, conv2_ref, qkv_weight_ref, out_weight_ref, *refs):
    parts, refs = refs[:-11], refs[-11:]
    output_ref, image_ref, act1_ref, hat2_ref, act2_ref, hat3_ref, qkv_ref, probs_ref, mixed_ref, stat_ref, p_ref = refs
    px, c = act1_ref.shape
    count = float(px * (c // GROUPS))
    spread = spread_ref[...]
    vec = lambda i: vec_ref[i : i + 1, :]
    gather(parts, image_ref)
    source = image_ref[...].astype(F32)
    m1, inv1 = norm_stats(source, spread, count)
    act1 = silu((source - m1) * (inv1 * vec(N1_GAIN)) + vec(N1_BIAS))
    act1_ref[...] = act1.astype(BF16)
    put_shifted(p_ref, act1, w)
    hidden1 = conv(p_ref, conv1_ref, px, w) + vec(PROJECTED)
    m2, inv2 = norm_stats(hidden1, spread, count)
    hat2 = (hidden1 - m2) * inv2
    hat2_ref[...] = hat2
    act2 = silu(hat2 * vec(N2_GAIN) + vec(N2_BIAS))
    act2_ref[...] = act2.astype(BF16)
    put_shifted(p_ref, act2, w)
    hidden2 = image_ref[...].astype(F32) + conv(p_ref, conv2_ref, px, w) + vec(C2_BIAS)
    m3, inv3 = norm_stats(hidden2, spread, count)
    stat_ref[...] = rows_of([m1, inv1, inv2, inv3], 8, c)
    hat3 = (hidden2 - m3) * inv3
    hat3_ref[...] = hat3
    normed3 = (hat3 * vec(N3_GAIN) + vec(N3_BIAS)).astype(BF16)
    qkv = mm(normed3, qkv_weight_ref[...])
    q = (qkv[:, :c] + vec(Q_BIAS)).astype(BF16)
    k = qkv[:, c : 2 * c].astype(BF16)
    v = qkv[:, 2 * c :].astype(BF16)
    qkv_ref[:, :c] = q
    qkv_ref[:, c : 2 * c] = k
    qkv_ref[:, 2 * c :] = v
    scores = mt(q, k) * c ** (-0.5)
    e = jnp.exp(scores - jnp.max(scores, axis=1, keepdims=True))
    probs = e * (1.0 / jnp.sum(e, axis=1, keepdims=True))
    probs_ref[...] = probs
    mixed = mm(probs.astype(BF16), v).astype(BF16)
    mixed_ref[...] = mixed
    output_ref[...] = (hidden2 + mm(mixed, out_weight_ref[...]) + vec(O_BIAS)).astype(BF16)


def main_kernel(w, vec_ref, spread_ref, qkv_weight_ref, out_weight_ref, act2_ref, hat3_ref, qkv_ref, probs_ref, mixed_ref, stat_ref, *refs):
    parts, (keep_ref, send_ref, small_ref, dh2_ref, q2_ref, cot_ref) = refs[:-6], refs[-6:]
    px, c = act2_ref.shape
    count = float(px * (c // GROUPS))
    scale = c ** (-0.5)
    spread = spread_ref[...]
    vec = lambda i: vec_ref[i : i + 1, :]
    gather(parts, cot_ref)
    cot = cot_ref[...]
    cot_wide = cot.astype(F32)
    probs = probs_ref[...]
    q, k, v = qkv_ref[:, :c], qkv_ref[:, c : 2 * c], qkv_ref[:, 2 * c :]
    put_halves(keep_ref, send_ref, 12 * c, tm(mixed_ref[...], cot))
    d_mixed = mt(cot, out_weight_ref[...]).astype(BF16)
    d_probs = mt(d_mixed, v)
    inner = jnp.sum(probs * d_probs, axis=1, keepdims=True)
    d_scores = (probs * (d_probs - inner)).astype(BF16)
    d_q = (mm(d_scores, k) * scale).astype(BF16)
    d_k = (tm(d_scores, q) * scale).astype(BF16)
    d_v = tm(probs.astype(BF16), d_mixed).astype(BF16)
    hat3 = hat3_ref[...]
    normed3_t = (hat3 * vec(N3_GAIN) + vec(N3_BIAS)).astype(BF16).T
    d_normed3 = None
    for i, d in enumerate((d_q, d_k, d_v)):
        put_halves(keep_ref, send_ref, (9 + i) * c, mm(normed3_t, d))
        part = mt(d, qkv_weight_ref[:, i * c : (i + 1) * c])
        d_normed3 = part if d_normed3 is None else d_normed3 + part
    d_src3, g_n3g, g_n3b = norm_back(d_normed3, hat3, stat_ref[3:4, :], vec(N3_GAIN), spread, count)
    d_hidden2 = cot_wide + d_src3
    dh2_ref[...] = d_hidden2
    put_shifted(q2_ref, d_hidden2, w)
    act2_t = act2_ref[...].T
    for tap in range(9):
        put_halves(keep_ref, send_ref, tap * c, tap_grad(act2_t, q2_ref, tap, px, w))
    sums = [g_n3g, g_n3b, col_sum(d_q.astype(F32)), col_sum(cot_wide), col_sum(d_hidden2)]
    small_ref[...] = rows_of(sums, 8, c)


def back_kernel(
    w, total, steps_ref, vec_ref, spread_ref, conv2_ref, act1_ref, hat2_ref, q2_ref, stat_ref, small_ref, keep_ref, send_ref, q1_ref,
):
    px, c = act1_ref.shape
    count = float(px * (c // GROUPS))
    spread = spread_ref[...]
    vec = lambda i: vec_ref[i : i + 1, :]
    hat2 = hat2_ref[...]
    d = conv_back(q2_ref, conv2_ref, px, w) * silu_slope(hat2 * vec(N2_GAIN) + vec(N2_BIAS))
    d_hidden1, g_n2g, g_n2b = norm_back(d, hat2, stat_ref[2:3, :], vec(N2_GAIN), spread, count)
    put_shifted(q1_ref, d_hidden1, w)
    act1_t = act1_ref[...].T
    for tap in range(9):
        put_halves(keep_ref, send_ref, tap * c, tap_grad(act1_t, q1_ref, tap, px, w))

    step = steps_ref[lax.axis_index("seq")]
    lane = lax.broadcasted_iota(jnp.int32, (1, c), 1) == device()
    digits = [jnp.where(lane, d, 0).astype(F32) for d in (step // DIGIT, step % DIGIT)]
    rows = [small_ref[i : i + 1, :] for i in range(5)] + [g_n2g, g_n2b] + digits
    own = lax.broadcasted_iota(jnp.int32, (total, c), 0) == device()
    sums = [rows_of(rows, VEC_ROWS, c), jnp.where(own, col_sum(d_hidden1), 0.0)]
    put_halves(keep_ref, send_ref, keep_ref.shape[0] - sums_rows(total), jnp.concatenate(sums, axis=0))


def source_kernel(
    w, vec_ref, spread_ref, conv1_ref, image_ref, dh2_ref, q1_ref, stat_ref, output_ref, token_ref, own_ref, *refs
):
    parts, grad_ref = refs[:-1], refs[-1]
    px, c = image_ref.shape
    count = float(px * (c // GROUPS))
    spread = spread_ref[...]
    vec = lambda i: vec_ref[i : i + 1, :]
    inv1 = stat_ref[1:2, :]
    hat1 = (image_ref[...].astype(F32) - stat_ref[0:1, :]) * inv1
    d = conv_back(q1_ref, conv1_ref, px, w) * silu_slope(hat1 * vec(N1_GAIN) + vec(N1_BIAS))
    d_src1, g_n1g, g_n1b = norm_back(d, hat1, inv1, vec(N1_GAIN), spread, count)
    grad_ref[...] = (dh2_ref[...] + d_src1).astype(BF16)
    for o, part in enumerate(parts):
        rows = at_rows(lax.axis_index("seq") ^ o, part.shape[1])
        part[0] = output_ref[rows, :]
        part[1] = grad_ref[rows, :]

    half = c // 2
    own_ref[...] = jnp.zeros(own_ref.shape, BF16)
    for i in range(2):
        rows = rows_of([g_n1g[:, i * half : (i + 1) * half], g_n1b[:, i * half : (i + 1) * half]], 16, half)
        own_ref[16 * i : 16 * i + 16, :] = rows.astype(BF16)


def add_kernel(step, groups, outputs, *refs):
    count = sum(g[0] for g in groups)
    outs = refs[count + 1 :]
    radix = step[1] if step else 1
    starts = [0] * len(outs)
    used = 0
    for i, (n, first, rows, whole) in enumerate(groups):
        ins = refs[used : used + n]
        used += n
        size = rows if whole else rows // radix
        targets = range(radix) if step else [0 if i < outputs[0] else 1]
        for o in targets:
            if step and not whole:
                where = pl.ds(pl.multiple_of(first + (digit(step) ^ o) * size, 16), size)
            else:
                where = slice(first, first + size)
            total = sum(r[where, :].astype(F32) for r in ins).astype(BF16)
            outs[o][starts[o] : starts[o] + size, :] = total
            starts[o] += size


def join_kernel(step, sizes, *refs):
    ins, outs = refs[: step[1]], refs[step[1] + 1 :]
    at = 0
    for out, parts in zip(outs, sizes):
        base = 0
        for rows in parts:
            size = rows // step[1]
            for o, part in enumerate(ins):
                where = base + (digit(step) ^ o) * size
                out[pl.ds(pl.multiple_of(where, 16), size), :] = part[at : at + size, :]
            base += rows
            at += size


class Writer:
    def __init__(self, sems):
        self.sems = sems
        self.copies = []

    def send(self, source, target):
        copy = pltpu.make_async_copy(source, target, self.sems.at[len(self.copies)])
        copy.start()
        self.copies.append(copy)

    def half(self, source, at, buffer, where, target, row, col):
        n = 2 * source.shape[1]
        buffer[where : where + n, :] = source[at : at + n, :].astype(F32)
        cols = pl.ds(pl.multiple_of(col, 128), source.shape[1])
        self.send(buffer.at[pl.ds(where, n)], target.at[pl.ds(row, n), cols])

    def more(self, source, core, buffer, conv2_hbm, qkv_hbm, out_hbm):
        c = out_hbm.shape[0]
        plan = [(conv2_hbm, tap * c, 0) for tap in range(EARLY_TAPS, 9)]
        plan += [(qkv_hbm, 0, i * c) for i in range(3)] + [(out_hbm, 0, 0)]
        for i, (target, row, col) in enumerate(plan):
            self.half(source, i * c, buffer, i * c, target, row, col + core * (c // 2))

    def first(self, source, start, core, buffer, at, conv1_hbm):
        c = conv1_hbm.shape[1]
        for tap in range(9):
            self.half(source, start + tap * c, buffer, at + tap * c, conv1_hbm, tap * c, core * (c // 2))

    def wait(self):
        for copy in self.copies:
            copy.wait()


def exact_tm(a, b):
    return tm(jnp.concatenate(a, axis=0).astype(BF16), jnp.concatenate(b, axis=0).astype(BF16))


def table_kernel(total, sums_ref, got_ref, table_ref, embed_ref, token_in, grad_table_hbm, grad_embed_hbm, *refs):
    vec_refs, token_ref = refs[:8], refs[8]
    grad_table_ref, grad_embed_ref, sems = refs[9:]
    token_ref[...] = jnp.zeros_like(token_ref)
    steps = table_ref.shape[0]
    writer = Writer(sems)
    left = device() & 1 == 0

    def take(row, rows):
        a, b = [ref[row : row + rows, :].astype(F32) for ref in (sums_ref, got_ref)]
        return jnp.where(left, a, b), jnp.where(left, b, a)

    d_proj = jnp.concatenate(take(VEC_ROWS, total), axis=1)
    rows = jnp.concatenate(take(0, VEC_ROWS), axis=1)
    both = rows[HIGH : HIGH + 1, :] * DIGIT + rows[LOW : LOW + 1, :]
    c = both.shape[1]
    own = lax.broadcasted_iota(jnp.int32, (total, c), 0) == lax.broadcasted_iota(jnp.int32, (total, c), 1)
    step = jnp.sum(jnp.where(own, both, 0.0), axis=1, keepdims=True).astype(jnp.int32)
    pick = jnp.where(lax.broadcasted_iota(jnp.int32, (total, steps), 1) == step, 1.0, 0.0)
    embedded = mm(pick.astype(BF16), table_ref[...])
    d_lifted = mt(d_proj.astype(BF16), embed_ref[...])
    d_embedded = d_lifted * silu_slope(embedded)
    pieces = three(d_embedded)
    for at in range(0, steps, 256):
        part = slice(at, min(at + 256, steps))
        grad_table_ref[part, :] = exact_tm([pick[:, part]] * 3, pieces)
        writer.send(grad_table_ref.at[part], grad_table_hbm.at[part])
    grad_embed_ref[...] = exact_tm(three(silu(embedded)), [d_proj] * 3)
    writer.send(grad_embed_ref, grad_embed_hbm)
    for i, ref in enumerate(vec_refs):
        ref[...] = col_sum(d_proj) if i == EB else rows[i : i + 1, :]
    writer.wait()


def early_kernel(own, mine_ref, got_ref, token_ref, conv2_hbm, gain_ref, bias_ref, out_token_ref, conv_ref, sems):
    c = conv2_hbm.shape[1]
    half = c // 2
    out_token_ref[...] = jnp.zeros_like(out_token_ref)
    at = mine_ref.shape[0] - own
    for i in range(2):
        rows = slice(at + 16 * i, at + 16 * i + 16)
        both = mine_ref[rows, :].astype(F32) + got_ref[rows, :].astype(F32)
        gain_ref[:, i * half : (i + 1) * half] = both[0:1, :]
        bias_ref[:, i * half : (i + 1) * half] = both[1:2, :]
    first = device() & 1 == 0
    writer = Writer(sems)
    for tap in range(EARLY_TAPS):
        rows = slice(tap * c, (tap + 1) * c)
        a, b = mine_ref[rows, :].astype(F32), got_ref[rows, :].astype(F32)
        conv_ref[rows, :half] = jnp.where(first, a, b)
        conv_ref[rows, half:] = jnp.where(first, b, a)
        writer.send(conv_ref.at[rows], conv2_hbm.at[rows])
    writer.wait()


def write_late(split, late_ref, core, buffer, sems, conv1_hbm, conv2_hbm, qkv_hbm, out_hbm):
    writer = Writer(sems)
    writer.more(late_ref, core, buffer, conv2_hbm, qkv_hbm, out_hbm)
    writer.first(late_ref, split, core, buffer, (13 - EARLY_TAPS) * out_hbm.shape[0], conv1_hbm)
    writer.wait()


def middle_kernel(split, late_ref, conv2_in, conv1_hbm, conv2_hbm, qkv_hbm, out_hbm, buffer, sems):
    write_late(split, late_ref, device() & 1, buffer, sems, conv1_hbm, conv2_hbm, qkv_hbm, out_hbm)


def last_kernel(split, late_ref, conv1_in, conv2_in, qkv_in, out_in, conv1_hbm, conv2_hbm, qkv_hbm, out_hbm, buffer, sems):
    write_late(split, late_ref, 1 - (device() & 1), buffer, sems, conv1_hbm, conv2_hbm, qkv_hbm, out_hbm)


def call(kernel, outs, specs, out_specs=None, scratch=(), limit=40, cost=1, aliases={}):
    return pl.pallas_call(
        kernel,
        out_shape=outs,
        in_specs=specs,
        out_specs=out_specs or [VMEM] * len(outs),
        scratch_shapes=scratch,
        input_output_aliases=aliases,
        compiler_params=pltpu.CompilerParams(vmem_limit_bytes=limit * 2**20),
        cost_estimate=pl.CostEstimate(flops=cost, bytes_accessed=1, transcendentals=0),
    )


def permute(array, partner, total):
    return lax.ppermute(array, AXES, [(i, partner(i)) for i in range(total)])


class Chain:
    def __init__(self, total, groups):
        self.total = total
        self.groups = groups

    def swap(self, array, low, offset):
        return permute(array, lambda i: i ^ (offset << low(i)), self.total)

    def add(self, step, token, cost=1, outputs=None):
        low, radix = step or (None, 1)
        flat = [p for g in self.groups for p in g[0]]
        sizes = [g[2] if g[3] else g[2] // radix for g in self.groups]
        outputs = outputs or [len(sizes)]
        cuts = [sum(sizes[: outputs[0]]), sum(sizes[outputs[0] :])][: len(outputs)]
        outs = [jax.ShapeDtypeStruct((n, flat[0].shape[1]), BF16) for n in (cuts if radix == 1 else cuts * radix)]
        groups = [(len(g[0]), g[1], g[2], g[3]) for g in self.groups]
        kernel = functools.partial(add_kernel, step, groups, outputs)
        outs = call(kernel, outs, [VMEM] * len(flat) + [ANY], cost=cost)(*flat, token)
        if len(outputs) > 1:
            self.parts = outs[:1]
            return outs
        self.parts = [outs[0]] + [self.swap(a, low, o + 1) for o, a in enumerate(outs[1:])]
        self.groups = [(self.parts, sum(sizes[:i]), n, g[3]) for i, (n, g) in enumerate(zip(sizes, self.groups))]
        return outs[0]

    def spread(self, step):
        low, radix = step
        self.parts = [self.parts[0]] + [self.swap(self.parts[0], low, o) for o in range(1, radix)]
        self.groups = [(self.parts,) + g[1:] for g in self.groups]

    def join(self, step, token, cost=1, sizes=None, every=False):
        rows, cols = self.parts[0].shape
        sizes = sizes or [[rows * step[1]]]
        outs = [jax.ShapeDtypeStruct((sum(n), cols), BF16) for n in sizes]
        kernel = functools.partial(join_kernel, step, sizes)
        self.parts = call(kernel, outs, [VMEM] * step[1] + [ANY], cost=cost)(*self.parts, token)
        return self.parts if every else self.parts[0]


def plan(total):
    bits = total.bit_length() - 1
    assert bits > 3 and 2**bits == total
    near = [(lambda i: 1 if i & 1 == 0 else 2, 2), (lambda i: 2 if i & 1 == 0 else 1, 2)]
    far = []
    low = 3
    while low < bits:
        take = min(2, bits - low)
        far.append((lambda i, low=low: low, 2**take))
        low += take
    return (lambda i: 0, 2), near, far


def shards(
    images, timesteps, step_table, norm1_gain, norm1_bias, conv1_weight, embed_weight, embed_bias,
    norm2_gain, norm2_bias, conv2_weight, conv2_bias, norm3_gain, norm3_bias, qkv_weight, query_bias,
    out_weight, out_bias, cotangent,
):
    maps, rows_here, w, c = images.shape
    seq = lax.axis_size("seq")
    total = lax.axis_size("dp") * seq
    assert maps == seq and total <= c
    px = rows_here * seq * w
    core, near, far = plan(total)
    shape = jax.ShapeDtypeStruct
    block = (maps, rows_here * w, c)
    pair = shape((2,) + block[1:], BF16)
    tiny = shape((8, c // 2), F32)
    field = lambda dtype: shape((px, c), dtype)
    shifted = (px + 2 * w, 3 * c)
    rows_a, rows_o, rows_v = padded(EARLY_TAPS * c, 2 * total), own_rows(total), sums_rows(total)
    rows_m, rows_1 = padded((13 - EARLY_TAPS) * c, 8 * total), padded(9 * c, 8 * total)
    conv1 = conv1_weight.reshape(9 * c, c)
    conv2 = conv2_weight.reshape(9 * c, c)

    def trade(parts):
        return [parts[0]] + [permute(p, lambda i, o=o + 1: i ^ o, total) for o, p in enumerate(parts[1:])]

    pieces = call(pack_kernel, [shape(block[1:], BF16)] * (2 * seq), [HBM] * 2, None, [pltpu.SemaphoreType.DMA((2 * seq,))], 54, EARLY_COST)(
        images.reshape(block), cotangent.reshape(block)
    )
    images_here, cots_here = trade(pieces[:seq]), trade(pieces[seq:])
    vectors = [norm1_gain, norm1_bias, norm2_gain, norm2_bias, conv2_bias, norm3_gain, norm3_bias, query_bias, out_bias, embed_bias]
    vec, spread = call(setup_kernel, [shape((16, c), F32), shape((c, c), BF16)], [SMEM] + [VMEM] * 2 + [ANY] * 2 + [VMEM] * 10, cost=EARLY_COST)(
        timesteps, step_table, embed_weight, conv1, conv2, *[v.reshape(1, c) for v in vectors]
    )
    half = lambda n: shape((n, c // 2), BF16)
    output, image, act1, hat2, *kept, stats = call(
        functools.partial(forward_kernel, w),
        [field(BF16), field(BF16), field(BF16), field(F32), field(BF16), field(F32), shape((px, 3 * c), BF16), field(F32), field(BF16)]
        + [shape((8, c), F32)],
        [VMEM] * (6 + seq),
        None,
        [pltpu.VMEM(shifted, BF16)],
    )(vec, spread, conv1, conv2, qkv_weight, out_weight, *images_here)
    keep_e, send_e, small, d_hidden2, q2 = call(
        functools.partial(main_kernel, w),
        [half(rows_a + rows_m)] * 2 + [shape((8, c), F32), field(F32), shape(shifted, BF16)],
        [VMEM] * (10 + seq),
        None,
        [pltpu.VMEM((px, c), BF16)],
    )(vec, spread, qkv_weight, out_weight, *kept, stats, *cots_here)
    swap = lambda array: permute(array, lambda i: i ^ 1, total)
    got_e = swap(send_e)
    keep_1, send_1, q1 = call(
        functools.partial(back_kernel, w, total), [half(rows_1 + rows_v)] * 2 + [shape(shifted, BF16)], [SMEM] + [VMEM] * 8
    )(timesteps, vec, spread, conv2, act1, hat2, q2, stats, small)
    got_1 = swap(send_1)
    m = Chain(total, [([keep_e, got_e], rows_a, rows_m, False)])
    token = m.add(near[0], q1)
    own, *results = call(
        functools.partial(source_kernel, w), [half(rows_o)] + [pair] * seq, [VMEM] * 8 + [ANY], None, [pltpu.VMEM((px, c), BF16)]
    )(vec, spread, conv1, image, d_hidden2, q1, stats, output, token)
    results = trade(results)
    f = Chain(total, [([keep_1, got_1], 0, rows_1, False)])
    a = Chain(total, [([keep_e, got_e], 0, rows_a, False), ([own], 0, rows_o, False), ([keep_1, got_1], rows_1, rows_v, True)])

    far_cuts = [1]
    for _, radix in far:
        far_cuts.append(far_cuts[-1] * radix)
    sizes_a = lambda cuts: [[rows_a // cuts, rows_o // cuts]]
    sizes_b = lambda cuts: [[rows_m // cuts, rows_1 // cuts]]
    token = f.add(near[0], results[0])
    token = a.add(far[0], token)
    token = m.add(None, token, SMALL_COST)
    b = Chain(total, m.groups + f.groups)
    token = b.add(near[1], token)
    for step in far[1:] + [None]:
        token = a.add(step, token, LONG_COST)
    token = b.add(far[0], token)
    token = a.add(None, token)
    a.spread(near[0])
    for step in far[1:] + [None]:
        token = b.add(step, token, SUM_COST)
    b.spread(far[-1])
    token = a.add(None, token)
    a.spread(near[1])
    output, grad_images, token = call(unpack_kernel, [shape(block, BF16)] * 2 + [tiny], [VMEM] * seq + [ANY], cost=UNPACK_COST)(*results, token)
    for i in range(len(far))[::-1]:
        token = b.join(far[i], token, LONG_COST, sizes_b(4 * far_cuts[i]))
        b.spread(far[i - 1] if i else near[1])
    token, sums = a.add(None, token, LONG_COST, [2, 1])
    a.spread(far[-1])
    token = b.join(near[1], token, 1, sizes_b(2))
    b.spread(near[0])
    outs = [shape(step_table.shape, F32), shape(embed_weight.shape, F32)]
    grad_table, grad_embed, *vecs, token = call(
        functools.partial(table_kernel, total),
        outs + [shape((1, c), F32)] * 8 + [tiny],
        [VMEM] * 4 + [ANY],
        [HBM] * 2 + [VMEM] * 9,
        [pltpu.VMEM(o.shape, F32) for o in outs] + [pltpu.SemaphoreType.DMA((1 + -(-step_table.shape[0] // 256),))],
    )(sums, swap(sums), step_table, embed_weight, token)
    for i in range(len(far))[::-1]:
        token = a.join(far[i], token, LONG_COST, sizes_a(far_cuts[i]))
        a.spread(far[i - 1] if i else core)
    grads = [shape((9 * c, c), F32), shape((9 * c, c), F32), shape(qkv_weight.shape, F32), shape(out_weight.shape, F32)]
    grad_conv2, grad_norm1_gain, grad_norm1_bias, token = call(
        functools.partial(early_kernel, rows_o),
        grads[:1] + [shape((1, c), F32)] * 2 + [tiny],
        [VMEM] * 2 + [ANY],
        [HBM] + [VMEM] * 3,
        [pltpu.VMEM((EARLY_TAPS * c, c), F32), pltpu.SemaphoreType.DMA((EARLY_TAPS,))],
    )(*a.parts, token)
    late = b.join(near[0], token, 1, sizes_b(1))
    got_late = swap(late)
    scratch = lambda blocks: [pltpu.VMEM((blocks * c, c // 2), F32), pltpu.SemaphoreType.DMA((blocks,))]
    count = 13 - EARLY_TAPS
    grads_half = call(
        functools.partial(middle_kernel, rows_m), grads, [VMEM] + [HBM], [HBM] * 4, scratch(count + 9), aliases={1: 1}
    )(late, grad_conv2)
    grad_conv1, grad_conv2, grad_qkv, grad_out = call(
        functools.partial(last_kernel, rows_m), grads, [VMEM] + [HBM] * 4, [HBM] * 4, scratch(count + 9), aliases={1: 0, 2: 1, 3: 2, 4: 3}
    )(got_late, *grads_half)
    one = lambda r: vecs[r].reshape(c)
    return (
        output.reshape(images.shape), grad_images.reshape(images.shape), grad_table, grad_norm1_gain.reshape(c), grad_norm1_bias.reshape(c),
        grad_conv1.reshape(conv1_weight.shape), grad_embed, one(EB), one(N2G), one(N2B), grad_conv2.reshape(conv2_weight.shape),
        one(C2B), one(N3G), one(N3B), grad_qkv, one(QB), grad_out, one(OB),
    )


def solution(mesh):
    field = P("dp", "seq", None, None)
    return jax.shard_map(
        shards,
        mesh=mesh,
        in_specs=(field, P("dp")) + (P(),) * 16 + (field,),
        out_specs=(field, field) + (P(),) * 16,
        check_vma=False,
    )
```
